256 devices in a mesh: blk: 256 (over z, y, x, core).
Axes of the slice: x: 4, y: 4, z: 8, core: 2. Of those that a mesh axis runs over, the one named last changes fastest.
Arguments:
- images: bfloat16 [196608, 1152], P('blk'), may hold values from -0.15 to 0.15
- texts: bfloat16 [196608, 1152], P('blk'), may hold values from -0.15 to 0.15
- log_scale: float32 [1], replicated, may hold values from 3 to 4.1
- logit_bias: float32 [1], replicated, may hold values from -4 to -1
Outputs:
- row_loss: float32 [196608], P('blk')
- image_grad: float32 [196608, 1152], P('blk')
- text_grad: float32 [196608, 1152], P('blk')
The draws below stay inside these ranges and needn't reach their ends.
All inputs are finite; a program needn't handle non-finite values.
Results may differ from the reference program's by a relative error of at most 0.0064.
Values may be sent and summed in bfloat16 or wider, within the bound.
No kernel may reach another device: no remote copies, remote signals or barrier semaphores. Data moves between devices by JAX's collectives and lax.ppermute only.
A program may use at most 64 MiB of HBM per device.

```python
import math
import jax
import jax.numpy as jnp
from jax import lax

D = 1152
RB = 768
STEPS = 3
BATCH = 196608
N_BLK = 256


def base_draw(key):
    normal_part = jnp.clip(jax.random.normal(jax.random.fold_in(key, 11), (BATCH, D), jnp.float32), -4.0, 4.0)
    return normal_part


def row_scales(key):
    return jnp.exp(jax.random.uniform(key, (BATCH, 1), jnp.float32, minval=math.log(0.02), maxval=math.log(0.2)))


def draw_images(key, part):
    shared = base_draw(key)
    key = jax.random.fold_in(key, 1)
    return (row_scales(key) * shared / math.sqrt(D)).astype(jnp.bfloat16)


def draw_texts(key, part):
    shared = base_draw(key)
    key = jax.random.fold_in(key, 2)
    noise = jnp.clip(jax.random.normal(jax.random.fold_in(key, 5), (BATCH, D), jnp.float32), -4.0, 4.0)
    mixed = 0.8 * shared + 0.6 * noise
    return (row_scales(jax.random.fold_in(key, 6)) * mixed / math.sqrt(D)).astype(jnp.bfloat16)


def setup_inputs(seed: int = 0) -> dict:
    splits = jax.random.split(jax.random.key(seed), 5)
    return {
        "images": draw_images(jax.random.fold_in(splits[4], 71), 0),
        "texts": draw_texts(jax.random.fold_in(splits[4], 71), 0),
        "log_scale": jnp.clip(jax.random.uniform(splits[2], (1,), jnp.float32, 3.0, 4.1), 3.0, 4.1),
        "logit_bias": jnp.clip(jax.random.uniform(splits[3], (1,), jnp.float32, -4.0, -1.0), -4.0, -1.0),
    }


EPS = 1e-12

def normalize(raw):
    widened = raw.astype(jnp.float32)
    inverse = lax.rsqrt(lax.optimization_barrier(jnp.sum(widened * widened, axis=1, keepdims=True)) + EPS)
    return (widened * inverse, inverse)

def score_block(image_block, text_block, scale_now, shift_now, own):
    rows = image_block.shape[0]
    products = lax.dot_general(image_block, text_block, (((1,), (1,)), ((), ())), preferred_element_type=jnp.float32)
    logits = scale_now * products + shift_now
    if own:
        row_ids = lax.broadcasted_iota(jnp.int32, logits.shape, 0)
        col_ids = lax.broadcasted_iota(jnp.int32, logits.shape, 1)
        labels = jnp.where(row_ids == col_ids, 1.0, -1.0).astype(jnp.float32)
    else:
        labels = -jnp.ones_like(logits)
    losses = jax.nn.softplus(-labels * logits)
    slopes = (-labels * jax.nn.sigmoid(-labels * logits) / rows).astype(jnp.bfloat16)
    return (losses, slopes)

def back_norm(unit, inverse, grad_unit):
    return (grad_unit - unit * lax.optimization_barrier(jnp.sum(unit * grad_unit, axis=1, keepdims=True))) * inverse

def reference(images, texts, log_scale, logit_bias):
    scale_now = jnp.exp(log_scale[0])
    shift_now = logit_bias[0]
    image_unit, image_inverse = normalize(images)
    text_unit, text_inverse = normalize(texts)
    blocks = N_BLK
    image_emb = image_unit.astype(jnp.bfloat16).reshape(blocks, RB, D)
    text_emb = text_unit.astype(jnp.bfloat16).reshape(blocks, RB, D)
    loss_sum = jnp.zeros((blocks, RB), jnp.float32)
    image_acc = jnp.zeros((blocks, RB, D), jnp.float32)
    text_acc = jnp.zeros((blocks, RB, D), jnp.float32)
    for offset in range(STEPS):
        rolled = jnp.roll(text_emb, offset, axis=0)

        def per_block(pair, own=offset == 0):
            image_block, text_block = pair
            losses, slopes = score_block(image_block, text_block, scale_now, shift_now, own)
            to_image = scale_now * jnp.dot(slopes, text_block, preferred_element_type=jnp.float32)
            to_text = scale_now * lax.dot_general(slopes, image_block, (((0,), (0,)), ((), ())), preferred_element_type=jnp.float32)
            return (lax.optimization_barrier(jnp.sum(losses, axis=1)), to_image, to_text)
        row_part, image_part, text_part = lax.map(per_block, (image_emb, rolled))
        loss_sum = loss_sum + row_part
        image_acc = image_acc + image_part
        text_acc = text_acc + jnp.roll(text_part, -offset, axis=0)
    row_loss = (loss_sum / (STEPS * RB)).reshape(blocks * RB)
    image_grad = back_norm(image_unit, image_inverse, image_acc.reshape(blocks * RB, D))
    text_grad = back_norm(text_unit, text_inverse, text_acc.reshape(blocks * RB, D))
    return (row_loss, image_grad, text_grad)
```

```python
import jax
import jax.numpy as jnp
from jax import lax
from jax.sharding import PartitionSpec as P

STEPS = 3
EPS = 1e-12


def normalize(raw):
    widened = raw.astype(jnp.float32)
    inverse = lax.rsqrt(jnp.sum(widened * widened, axis=1, keepdims=True) + EPS)
    return (widened * inverse, inverse)


def back_norm(unit, inverse, grad_unit):
    return (grad_unit - unit * jnp.sum(unit * grad_unit, axis=1, keepdims=True)) * inverse


def logits_of(image_emb, text_emb, scale_now, shift_now):
    products = lax.dot_general(
        image_emb, text_emb, (((1,), (1,)), ((), ())), preferred_element_type=jnp.float32
    )
    return scale_now * products + shift_now


def slopes_of(logits, labels, rows):
    return (-labels * jax.nn.sigmoid(-labels * logits) / rows).astype(jnp.bfloat16)


def per_device(images, texts, log_scale, logit_bias):
    count = lax.axis_size("blk")
    odd = lax.axis_index("blk") % 2 == 1
    scale_now = jnp.exp(log_scale[0])
    shift_now = logit_bias[0]
    rows = images.shape[0]

    def send(block, pairs):
        return lax.ppermute(block, "blk", pairs)

    up = [(i, (i + 2) % count) for i in range(count)]
    down = [(i, (i - 2) % count) for i in range(count)]
    across = [(i, i ^ 1) for i in range(count)]
    texts_two = send(texts, up)
    images_two = send(images, down)
    early = send(jnp.where(odd, images, texts), across)
    late = send(jnp.where(odd, texts_two, images_two), across)
    texts_one = jnp.where(odd, early, late)
    images_one = jnp.where(odd, late, early)

    image_unit, image_inverse = normalize(images)
    text_unit, text_inverse = normalize(texts)
    image_emb = image_unit.astype(jnp.bfloat16)
    text_emb = text_unit.astype(jnp.bfloat16)

    logits = logits_of(image_emb, text_emb, scale_now, shift_now)
    labels = jnp.where(jnp.eye(rows, dtype=bool), 1.0, -1.0).astype(jnp.float32)
    loss = jnp.sum(jax.nn.softplus(-labels * logits), axis=1)
    slopes = slopes_of(logits, labels, rows)
    image_acc = scale_now * jnp.dot(slopes, text_emb, preferred_element_type=jnp.float32)
    text_acc = scale_now * lax.dot_general(
        slopes, image_emb, (((0,), (0,)), ((), ())), preferred_element_type=jnp.float32
    )
    for other in (texts_one, texts_two):
        emb = normalize(other)[0].astype(jnp.bfloat16)
        logits = logits_of(image_emb, emb, scale_now, shift_now)
        loss = loss + jnp.sum(jax.nn.softplus(logits), axis=1)
        image_acc = image_acc + scale_now * jnp.dot(
            slopes_of(logits, -1.0, rows), emb, preferred_element_type=jnp.float32
        )
    for other in (images_one, images_two):
        emb = normalize(other)[0].astype(jnp.bfloat16)
        logits = logits_of(text_emb, emb, scale_now, shift_now)
        text_acc = text_acc + scale_now * jnp.dot(
            slopes_of(logits, -1.0, rows), emb, preferred_element_type=jnp.float32
        )
    row_loss = loss / (STEPS * rows)
    return (
        row_loss,
        back_norm(image_unit, image_inverse, image_acc),
        back_norm(text_unit, text_inverse, text_acc),
    )


def solution(mesh):
    placed = (P("blk", None), P("blk", None), P(), P())
    return jax.shard_map(
        per_device,
        mesh=mesh,
        in_specs=placed,
        out_specs=(P("blk"), P("blk", None), P("blk", None)),
        check_vma=False,
    )
```

```python
import functools

import jax
import jax.numpy as jnp
from jax import lax
from jax.experimental import pallas as pl
from jax.experimental.pallas import tpu as pltpu
from jax.sharding import PartitionSpec as P

STEPS = 3
EPS = 1e-12
RB = 768
D = 1152
TILE = 256
LANES = 128
PARTS = RB // TILE
VMEM_LIMIT = 12 * 1024 * 1024
CUT = 512
NEAR, FAR = 0, 1

ROWS_BY_COLS = (((1,), (1,)), ((), ()))
TRANSPOSED = (((0,), (0,)), ((), ()))

SCALARS = pl.BlockSpec(memory_space=pltpu.SMEM)
RESIDENT = pl.BlockSpec(memory_space=pltpu.VMEM)
ANYWHERE = pl.BlockSpec(memory_space=pl.ANY)
NO_COST = pl.CostEstimate(flops=1, bytes_accessed=1, transcendentals=0)


def kept(array):
    return pltpu.with_memory_space_constraint(array, pltpu.VMEM)


def tile(part):
    return slice(part * TILE, (part + 1) * TILE)


def normalize(raw):
    widened = raw.astype(jnp.float32)
    inverse = lax.rsqrt(jnp.sum(widened * widened, axis=1, keepdims=True) + EPS)
    return (widened * inverse, inverse)


def matmul(a, b, dims=(((1,), (0,)), ((), ()))):
    return lax.dot_general(a, b, dims, preferred_element_type=jnp.float32)


def scale_row(log_scale, width):
    return jnp.exp(jnp.full((1, width), log_scale[0], jnp.float32))


def lane_sums(values):
    total = values[:, :LANES]
    for start in range(LANES, values.shape[1], LANES):
        total = total + values[:, start : start + LANES]
    return total


def softplus_and_slope(signed):
    raised = jnp.exp(signed)
    slope = raised / ((1.0 + raised) * RB)
    return jnp.log1p(raised), slope


def pick_kernel(odd, images, texts, far, near_head, near_tail, sems):
    def copies(far_block, near_block):
        return [
            pltpu.make_async_copy(far_block, far, sems.at[0]),
            pltpu.make_async_copy(near_block.at[pl.ds(0, CUT)], near_head, sems.at[1]),
            pltpu.make_async_copy(near_block.at[pl.ds(CUT, RB - CUT)], near_tail, sems.at[2]),
        ]

    @pl.when(odd[0] == 1)
    def _():
        for copy in copies(texts, images):
            copy.start()

    @pl.when(odd[0] == 0)
    def _():
        for copy in copies(images, texts):
            copy.start()

    for copy in copies(images, texts):
        copy.wait()


def pick(odd, images, texts):
    return pl.pallas_call(
        pick_kernel,
        in_specs=[SCALARS, ANYWHERE, ANYWHERE],
        out_specs=[RESIDENT] * 3,
        out_shape=[
            pltpu.VMEM((RB, D), jnp.bfloat16),
            pltpu.VMEM((CUT, D), jnp.bfloat16),
            pltpu.VMEM((RB - CUT, D), jnp.bfloat16),
        ],
        scratch_shapes=[pltpu.SemaphoreType.DMA((3,))],
        cost_estimate=NO_COST,
        name="pick",
    )(
        odd,
        pltpu.with_memory_space_constraint(images, pltpu.HBM),
        pltpu.with_memory_space_constraint(texts, pltpu.HBM),
    )


def embed(raw):
    return normalize(raw)[0].astype(jnp.bfloat16)


def prepare_kernel(far, near_head, near_tail, emb):
    for part in range(PARTS):
        emb[FAR, tile(part)] = embed(far[tile(part)])
    for part in range(CUT // TILE):
        emb[NEAR, tile(part)] = embed(near_head[tile(part)])
    emb[NEAR, CUT:] = embed(near_tail[...])


def prepare(far, near_head, near_tail):
    return pl.pallas_call(
        prepare_kernel,
        in_specs=[RESIDENT] * 3,
        out_specs=RESIDENT,
        out_shape=pltpu.VMEM((2, RB, D), jnp.bfloat16),
        compiler_params=pltpu.CompilerParams(vmem_limit_bytes=VMEM_LIMIT),
        cost_estimate=NO_COST,
        name="prepare",
    )(kept(far), kept(near_head), kept(near_tail))


def own_kernel(odd, log_scale, logit_bias, emb, grads, loss, slopes):
    scale_tile, scale_wide = scale_row(log_scale, TILE), scale_row(log_scale, D)
    row_ids = lax.broadcasted_iota(jnp.int32, (TILE, TILE), 0)
    col_ids = lax.broadcasted_iota(jnp.int32, (TILE, TILE), 1)
    images, texts = 1 - odd[0], odd[0]
    for row in range(PARTS):
        losses = jnp.zeros((TILE, LANES), jnp.float32)
        for col in range(PARTS):
            logits = (
                scale_tile * matmul(emb[images, tile(row)], emb[texts, tile(col)], ROWS_BY_COLS)
                + logit_bias[0]
            )
            if row == col:
                same = row_ids == col_ids
                terms, slope = softplus_and_slope(jnp.where(same, -logits, logits))
                slope = jnp.where(same, -slope, slope)
            else:
                terms, slope = softplus_and_slope(logits)
            losses = losses + lane_sums(terms)
            slopes[tile(row), tile(col)] = slope.astype(jnp.bfloat16)
        loss[tile(row)] = losses
        grads[images, tile(row)] = scale_wide * matmul(slopes[tile(row)], emb[texts])
    for col in range(PARTS):
        grads[texts, tile(col)] = scale_wide * matmul(
            slopes[:, tile(col)], emb[images], TRANSPOSED
        )


def own_pairs(odd, log_scale, logit_bias, emb):
    return pl.pallas_call(
        own_kernel,
        in_specs=[SCALARS] * 3 + [RESIDENT],
        out_specs=[RESIDENT] * 2,
        out_shape=[
            pltpu.VMEM((2, RB, D), jnp.float32),
            pltpu.VMEM((RB, LANES), jnp.float32),
        ],
        scratch_shapes=[pltpu.VMEM((RB, RB), jnp.bfloat16)],
        compiler_params=pltpu.CompilerParams(vmem_limit_bytes=VMEM_LIMIT),
        cost_estimate=NO_COST,
        name="own_pairs",
    )(odd, log_scale, logit_bias, kept(emb))


def embed_all(others, other_emb):
    start = 0
    for other in others:
        for part in range(other.shape[0] // TILE):
            other_emb[start : start + TILE] = embed(other[tile(part)])
            start += TILE


def score(row, side, has_loss, log_scale, logit_bias, emb, loss_in, loss, other_emb, slopes):
    scale_tile = scale_row(log_scale, TILE)
    losses = jnp.zeros((TILE, LANES), jnp.float32)
    for col in range(other_emb.shape[0] // TILE):
        logits = (
            scale_tile * matmul(emb[side, tile(row)], other_emb[tile(col)], ROWS_BY_COLS)
            + logit_bias[0]
        )
        terms, slope = softplus_and_slope(logits)
        losses = losses + lane_sums(terms)
        slopes[tile(row), tile(col)] = slope.astype(jnp.bfloat16)
    loss[tile(row)] = loss_in[tile(row)] + jnp.where(has_loss, losses, 0.0)
    return scale_row(log_scale, D) * matmul(slopes[tile(row)], other_emb[...])


def add_kernel(*refs, side, pieces):
    odd, log_scale, logit_bias, *others = refs[: 3 + pieces]
    emb, grads_in, loss_in, grads, loss, other_emb, slopes = refs[3 + pieces :]
    embed_all(others, other_emb)
    has_loss = odd[0] == (1 if side == NEAR else 0)
    for row in range(PARTS):
        addend = score(
            row, side, has_loss, log_scale, logit_bias, emb, loss_in, loss, other_emb, slopes
        )
        grads[side, tile(row)] = grads_in[side, tile(row)] + addend


def finish_kernel(*refs, side, raws):
    odd, log_scale, logit_bias, other, emb, grads, loss_in = refs[:7]
    raw = refs[7 : 7 + raws]
    tail = refs[7 + raws + (2 if side == FAR else 0) :]
    result, image_grad, text_grad, other_emb, slopes, finished, sems = tail
    embed_all([other], other_emb)
    has_loss = odd[0] == (1 if side == NEAR else 0)
    loss = result
    for row in range(PARTS):
        here = tile(row)
        addend = score(
            row, side, has_loss, log_scale, logit_bias, emb, loss_in, loss, other_emb, slopes
        )
        total = grads[side, here] + addend
        if raws == 1:
            mine = raw[0][here]
        else:
            mine = raw[0][here] if row * TILE < CUT else raw[1][tile(row - CUT // TILE)]
        unit, inverse = normalize(mine)
        finished[here] = (total - unit * jnp.sum(unit * total, axis=1, keepdims=True)) * inverse

        @pl.when(odd[0] == (1 if side == NEAR else 0))
        def _(here=here, row=row):
            pltpu.make_async_copy(finished.at[here], image_grad.at[here], sems.at[row]).start()

        @pl.when(odd[0] == (0 if side == NEAR else 1))
        def _(here=here, row=row):
            pltpu.make_async_copy(finished.at[here], text_grad.at[here], sems.at[row]).start()

    for row in range(PARTS):
        here = tile(row)
        pltpu.make_async_copy(finished.at[here], image_grad.at[here], sems.at[row]).wait()


def score_scratch(count):
    return [pltpu.VMEM((count, D), jnp.bfloat16), pltpu.VMEM((RB, count), jnp.bfloat16)]


def add_pairs(side, scalars, others, emb, grads, loss):
    count = sum(other.shape[0] for other in others)
    at = 4 + len(others)
    return pl.pallas_call(
        functools.partial(add_kernel, side=side, pieces=len(others)),
        in_specs=[SCALARS] * 3 + [RESIDENT] * (3 + len(others)),
        out_specs=[RESIDENT] * 2,
        out_shape=[
            pltpu.VMEM(grads.shape, jnp.float32),
            pltpu.VMEM(loss.shape, jnp.float32),
        ],
        scratch_shapes=score_scratch(count),
        input_output_aliases={at: 0, at + 1: 1},
        compiler_params=pltpu.CompilerParams(vmem_limit_bytes=VMEM_LIMIT),
        cost_estimate=NO_COST,
        name="add_pairs",
    )(*scalars, *map(kept, others), kept(emb), kept(grads), kept(loss))


def finish_pairs(side, scalars, other, emb, grads, loss, raws, outs=()):
    count = other.shape[0]
    aliases = {6: 0}
    if outs:
        aliases |= {7 + len(raws): 1, 8 + len(raws): 2}
    return pl.pallas_call(
        functools.partial(finish_kernel, side=side, raws=len(raws)),
        in_specs=[SCALARS] * 3 + [RESIDENT] * (4 + len(raws)) + [ANYWHERE] * len(outs),
        out_specs=[RESIDENT, ANYWHERE, ANYWHERE],
        out_shape=[
            pltpu.VMEM(loss.shape, jnp.float32),
            jax.ShapeDtypeStruct((RB, D), jnp.float32),
            jax.ShapeDtypeStruct((RB, D), jnp.float32),
        ],
        scratch_shapes=score_scratch(count)
        + [
            pltpu.VMEM((RB, D), jnp.float32),
            pltpu.SemaphoreType.DMA((PARTS,)),
        ],
        input_output_aliases=aliases,
        compiler_params=pltpu.CompilerParams(vmem_limit_bytes=VMEM_LIMIT),
        cost_estimate=NO_COST,
        name="finish_pairs",
    )(*scalars, kept(other), kept(emb), kept(grads), kept(loss), *map(kept, raws), *outs)


def per_device(images, texts, log_scale, logit_bias):
    count = lax.axis_size("blk")
    odd = (lax.axis_index("blk") % 2).astype(jnp.int32)[None]
    scalars = (odd, log_scale, logit_bias)

    first = [(i, (i + 2) % count if i % 2 else (i - 2) % count) for i in range(count)]
    second = [(i, (i + 1) % count if i % 2 else (i - 1) % count) for i in range(count)]
    across = [(i, i ^ 1) for i in range(count)]

    def send(block, pairs):
        return lax.ppermute(block, "blk", pairs)

    far, near_head, near_tail = pick(odd, images, texts)
    far_other = send(far, first)
    beside_head = send(near_head, across)
    beside_tail = send(near_tail, across)
    emb = prepare(far, near_head, near_tail)
    beside_head, beside_tail, emb = lax.optimization_barrier((beside_head, beside_tail, emb))
    near_head_other = send(beside_head, second)
    near_tail_other = send(beside_tail, second)
    grads, loss = own_pairs(*scalars, emb)
    grads, loss = add_pairs(NEAR, scalars, [beside_head, beside_tail], emb, grads, loss)
    far_other, grads = lax.optimization_barrier((far_other, grads))
    far_beside = [send(far_other[start : start + TILE], across) for start in range(0, RB, TILE)]
    loss, *outs = finish_pairs(
        NEAR, scalars, far_other, emb, grads, loss, [near_head, near_tail]
    )
    grads, loss = add_pairs(FAR, scalars, far_beside, emb, grads, loss)
    grads, loss = add_pairs(FAR, scalars, [near_head_other], emb, grads, loss)
    loss, image_grad, text_grad = finish_pairs(
        FAR, scalars, near_tail_other, emb, grads, loss, [far], outs
    )
    row_loss = jnp.sum(loss, axis=1) / (STEPS * RB)
    return (row_loss, image_grad, text_grad)


def solution(mesh):
    placed = (P("blk", None), P("blk", None), P(), P())
    return jax.shard_map(
        per_device,
        mesh=mesh,
        in_specs=placed,
        out_specs=(P("blk"), P("blk", None), P("blk", None)),
        check_vma=False,
    )
```

```python
import functools

import jax
import jax.numpy as jnp
from jax import lax
from jax.experimental import pallas as pl
from jax.experimental.pallas import tpu as pltpu
from jax.sharding import PartitionSpec as P

STEPS = 3
EPS = 1e-12
RB = 768
D = 1152
TILE = 256
LANES = 128
PARTS = RB // TILE
VMEM_LIMIT = 12 * 1024 * 1024
CUT = 400
PIECE = 256
NEAR, FAR = 0, 1

ROWS_BY_COLS = (((1,), (1,)), ((), ()))
TRANSPOSED = (((0,), (0,)), ((), ()))

SCALARS = pl.BlockSpec(memory_space=pltpu.SMEM)
RESIDENT = pl.BlockSpec(memory_space=pltpu.VMEM)
ANYWHERE = pl.BlockSpec(memory_space=pl.ANY)
NO_COST = pl.CostEstimate(flops=1, bytes_accessed=1, transcendentals=0)


def kept(array):
    return pltpu.with_memory_space_constraint(array, pltpu.VMEM)


def in_hbm(array):
    return pltpu.with_memory_space_constraint(array, pltpu.HBM)


def tile(part):
    return slice(part * TILE, (part + 1) * TILE)


def normalize(raw):
    widened = raw.astype(jnp.float32)
    inverse = lax.rsqrt(jnp.sum(widened * widened, axis=1, keepdims=True) + EPS)
    return (widened * inverse, inverse)


def matmul(a, b, dims=(((1,), (0,)), ((), ()))):
    return lax.dot_general(a, b, dims, preferred_element_type=jnp.float32)


def scale_row(log_scale, width):
    return jnp.exp(jnp.full((1, width), log_scale[0], jnp.float32))


def lane_sums(values):
    total = values[:, :LANES]
    for start in range(LANES, values.shape[1], LANES):
        total = total + values[:, start : start + LANES]
    return total


def softplus_and_slope(signed):
    raised = jnp.exp(signed)
    slope = raised / ((1.0 + raised) * RB)
    return jnp.log1p(raised), slope


def copy_if(condition, source, target, sem):
    @pl.when(condition)
    def _():
        pltpu.make_async_copy(source, target, sem).start()


def pick_kernel(odd, images, texts, far, sem):
    copy_if(odd[0] == 1, texts, far, sem)
    copy_if(odd[0] == 0, images, far, sem)
    pltpu.make_async_copy(images, far, sem).wait()


def pick(odd, images, texts):
    return pl.pallas_call(
        pick_kernel,
        in_specs=[SCALARS, ANYWHERE, ANYWHERE],
        out_specs=RESIDENT,
        out_shape=pltpu.VMEM((RB, D), jnp.bfloat16),
        scratch_shapes=[pltpu.SemaphoreType.DMA],
        cost_estimate=NO_COST,
        name="pick",
    )(odd, in_hbm(images), in_hbm(texts))


def embed(raw):
    return normalize(raw)[0].astype(jnp.bfloat16)


def prepare_kernel(odd, images, texts, far, emb, near_head, near_tail, sems):
    head, tail = pl.ds(0, CUT), pl.ds(CUT, RB - CUT)
    copy_if(odd[0] == 1, images.at[head], near_head, sems.at[0])
    copy_if(odd[0] == 0, texts.at[head], near_head, sems.at[0])
    copy_if(odd[0] == 1, images.at[tail], near_tail, sems.at[1])
    copy_if(odd[0] == 0, texts.at[tail], near_tail, sems.at[1])
    for part in range(PARTS):
        emb[FAR, tile(part)] = embed(far[tile(part)])
    pltpu.make_async_copy(images.at[head], near_head, sems.at[0]).wait()
    pltpu.make_async_copy(images.at[tail], near_tail, sems.at[1]).wait()
    emb[NEAR, :CUT] = embed(near_head[...])
    emb[NEAR, CUT:] = embed(near_tail[...])


def prepare(odd, images, texts, far):
    return pl.pallas_call(
        prepare_kernel,
        in_specs=[SCALARS, ANYWHERE, ANYWHERE, RESIDENT],
        out_specs=[RESIDENT] * 3,
        out_shape=[
            pltpu.VMEM((2, RB, D), jnp.bfloat16),
            pltpu.VMEM((CUT, D), jnp.bfloat16),
            pltpu.VMEM((RB - CUT, D), jnp.bfloat16),
        ],
        scratch_shapes=[pltpu.SemaphoreType.DMA((2,))],
        compiler_params=pltpu.CompilerParams(vmem_limit_bytes=VMEM_LIMIT),
        cost_estimate=NO_COST,
        name="prepare",
    )(odd, in_hbm(images), in_hbm(texts), kept(far))


def own_kernel(odd, log_scale, logit_bias, emb, grads, loss, slopes):
    scale_tile, scale_wide = scale_row(log_scale, TILE), scale_row(log_scale, D)
    row_ids = lax.broadcasted_iota(jnp.int32, (TILE, TILE), 0)
    col_ids = lax.broadcasted_iota(jnp.int32, (TILE, TILE), 1)
    images, texts = 1 - odd[0], odd[0]
    for row in range(PARTS):
        losses = jnp.zeros((TILE, LANES), jnp.float32)
        for col in range(PARTS):
            logits = (
                scale_tile * matmul(emb[images, tile(row)], emb[texts, tile(col)], ROWS_BY_COLS)
                + logit_bias[0]
            )
            if row == col:
                same = row_ids == col_ids
                terms, slope = softplus_and_slope(jnp.where(same, -logits, logits))
                slope = jnp.where(same, -slope, slope)
            else:
                terms, slope = softplus_and_slope(logits)
            losses = losses + lane_sums(terms)
            slopes[tile(row), tile(col)] = slope.astype(jnp.bfloat16)
        loss[tile(row)] = losses
        grads[images, tile(row)] = scale_wide * matmul(slopes[tile(row)], emb[texts])
    for col in range(PARTS):
        grads[texts, tile(col)] = scale_wide * matmul(
            slopes[:, tile(col)], emb[images], TRANSPOSED
        )


def own_pairs(odd, log_scale, logit_bias, emb):
    return pl.pallas_call(
        own_kernel,
        in_specs=[SCALARS] * 3 + [RESIDENT],
        out_specs=[RESIDENT] * 2,
        out_shape=[
            pltpu.VMEM((2, RB, D), jnp.float32),
            pltpu.VMEM((RB, LANES), jnp.float32),
        ],
        scratch_shapes=[pltpu.VMEM((RB, RB), jnp.bfloat16)],
        compiler_params=pltpu.CompilerParams(vmem_limit_bytes=VMEM_LIMIT),
        cost_estimate=NO_COST,
        name="own_pairs",
    )(odd, log_scale, logit_bias, kept(emb))


def padded(count):
    return -(-count // LANES) * LANES


def embed_all(others, other_emb):
    start = 0
    for other in others:
        count = other.shape[0]
        for at in range(0, count, LANES):
            step = min(LANES, count - at)
            other_emb[start : start + step] = embed(other[at : at + step])
            start += step
    if start < other_emb.shape[0]:
        other_emb[start:] = jnp.zeros((other_emb.shape[0] - start, D), jnp.bfloat16)
    return start


def score(side, has_loss, log_scale, logit_bias, emb, loss_in, loss, other_emb, slopes, valid):
    count = other_emb.shape[0]
    step = RB if count == RB else TILE
    for row in range(0, RB, step):
        rows = slice(row, row + step)
        losses = jnp.zeros((step, LANES), jnp.float32)
        for start in range(0, count, TILE):
            cols = slice(start, min(start + TILE, count))
            width = cols.stop - start
            logits = (
                scale_row(log_scale, width)
                * matmul(emb[side, rows], other_emb[cols], ROWS_BY_COLS)
                + logit_bias[0]
            )
            terms, slope = softplus_and_slope(logits)
            if cols.stop > valid:
                ids = lax.broadcasted_iota(jnp.int32, (step, width), 1)
                terms = jnp.where(ids < valid - start, terms, 0.0)
            losses = losses + lane_sums(terms)
            slopes[rows, cols] = slope.astype(jnp.bfloat16)
        loss[rows] = loss_in[rows] + jnp.where(has_loss, losses, 0.0)


def add_kernel(*refs, side, pieces):
    odd, log_scale, logit_bias, *others = refs[: 3 + pieces]
    emb, grads_in, loss_in, grads, loss, other_emb, slopes = refs[3 + pieces :]
    valid = embed_all(others, other_emb)
    has_loss = odd[0] == (1 if side == NEAR else 0)
    score(side, has_loss, log_scale, logit_bias, emb, loss_in, loss, other_emb, slopes, valid)
    scale_wide = scale_row(log_scale, D)
    step = RB if other_emb.shape[0] == RB else TILE
    for row in range(0, RB, step):
        rows = slice(row, row + step)
        grads[side, rows] = grads_in[side, rows] + scale_wide * matmul(
            slopes[rows], other_emb[...]
        )


def finish_kernel(*refs, side):
    odd, log_scale, logit_bias, other, emb, grads, loss_in, images, texts = refs[:9]
    if side == FAR:
        refs = refs[2:]
    loss, image_grad, text_grad, *scratch = refs[9:]
    other_emb, slopes, raw, finished, raw_sem, out_sems = scratch[:6]
    of_images = odd[0] == (1 if side == NEAR else 0)
    copy_if(of_images, images, raw, raw_sem)
    copy_if(jnp.logical_not(of_images), texts, raw, raw_sem)
    valid = embed_all([other], other_emb)
    sums = loss if side == NEAR else scratch[6]
    score(side, of_images, log_scale, logit_bias, emb, loss_in, sums, other_emb, slopes, valid)
    scale_wide = scale_row(log_scale, D)

    def accumulate(rows):
        finished[rows] = grads[side, rows] + scale_wide * matmul(slopes[rows], other_emb[...])

    def finish(here):
        total = finished[here]
        unit, inverse = normalize(raw[here])
        finished[here] = (total - unit * jnp.sum(unit * total, axis=1, keepdims=True)) * inverse

    if side == NEAR:
        accumulate(slice(0, RB))
    pltpu.make_async_copy(images, raw, raw_sem).wait()
    for row in range(PARTS):
        here = tile(row)
        if side == FAR:
            accumulate(here)
        finish(here)
        copy_if(of_images, finished.at[here], image_grad.at[here], out_sems.at[row])
        copy_if(
            jnp.logical_not(of_images), finished.at[here], text_grad.at[here], out_sems.at[row]
        )
    if side == FAR:
        for row in range(PARTS):
            loss[tile(row)] = jnp.sum(sums[tile(row)].T, axis=0) * (1.0 / (STEPS * RB))
    for row in range(PARTS):
        here = tile(row)
        pltpu.make_async_copy(finished.at[here], image_grad.at[here], out_sems.at[row]).wait()


def score_scratch(count):
    return [
        pltpu.VMEM((padded(count), D), jnp.bfloat16),
        pltpu.VMEM((RB, padded(count)), jnp.bfloat16),
    ]


def add_pairs(side, scalars, others, emb, grads, loss):
    count = sum(other.shape[0] for other in others)
    at = 4 + len(others)
    return pl.pallas_call(
        functools.partial(add_kernel, side=side, pieces=len(others)),
        in_specs=[SCALARS] * 3 + [RESIDENT] * (3 + len(others)),
        out_specs=[RESIDENT] * 2,
        out_shape=[
            pltpu.VMEM(grads.shape, jnp.float32),
            pltpu.VMEM(loss.shape, jnp.float32),
        ],
        scratch_shapes=score_scratch(count),
        input_output_aliases={at: 0, at + 1: 1},
        compiler_params=pltpu.CompilerParams(vmem_limit_bytes=VMEM_LIMIT),
        cost_estimate=NO_COST,
        name="add_pairs",
    )(*scalars, *map(kept, others), kept(emb), kept(grads), kept(loss))


def finish_pairs(side, scalars, other, emb, grads, loss, images, texts, outs=()):
    count = other.shape[0]
    last = side == FAR
    return pl.pallas_call(
        functools.partial(finish_kernel, side=side),
        in_specs=[SCALARS] * 3 + [RESIDENT] * 4 + [ANYWHERE] * (2 + len(outs)),
        out_specs=[RESIDENT, ANYWHERE, ANYWHERE],
        out_shape=[
            jax.ShapeDtypeStruct((RB,), jnp.float32)
            if last
            else pltpu.VMEM(loss.shape, jnp.float32),
            jax.ShapeDtypeStruct((RB, D), jnp.float32),
            jax.ShapeDtypeStruct((RB, D), jnp.float32),
        ],
        scratch_shapes=score_scratch(count)
        + [
            pltpu.VMEM((RB, D), jnp.bfloat16),
            pltpu.VMEM((RB, D), jnp.float32),
            pltpu.SemaphoreType.DMA,
            pltpu.SemaphoreType.DMA((PARTS,)),
        ]
        + ([pltpu.VMEM(loss.shape, jnp.float32)] if last else []),
        input_output_aliases={9: 1, 10: 2} if last else {6: 0},
        compiler_params=pltpu.CompilerParams(vmem_limit_bytes=VMEM_LIMIT),
        cost_estimate=NO_COST,
        name="finish_pairs",
    )(
        *scalars,
        kept(other),
        kept(emb),
        kept(grads),
        kept(loss),
        in_hbm(images),
        in_hbm(texts),
        *outs,
    )


def per_device(images, texts, log_scale, logit_bias):
    count = lax.axis_size("blk")
    odd = (lax.axis_index("blk") % 2).astype(jnp.int32)[None]
    scalars = (odd, log_scale, logit_bias)

    first = [(i, (i + 2) % count if i % 2 else (i - 2) % count) for i in range(count)]
    second = [(i, (i + 1) % count if i % 2 else (i - 1) % count) for i in range(count)]
    across = [(i, i ^ 1) for i in range(count)]

    def send(block, pairs):
        return lax.ppermute(block, "blk", pairs)

    far = pick(odd, images, texts)
    far_other = send(far, first)
    emb, near_head, near_tail = prepare(odd, images, texts, far)
    beside_head = send(near_head, across)
    beside_tail = send(near_tail, across)
    beside_head, beside_tail, emb = lax.optimization_barrier((beside_head, beside_tail, emb))
    near_head_other = send(beside_head, second)
    grads, loss = own_pairs(*scalars, emb)
    beside_tail, grads = lax.optimization_barrier((beside_tail, grads))
    near_tail_other = send(beside_tail, second)
    grads, loss = add_pairs(NEAR, scalars, [beside_head, beside_tail], emb, grads, loss)
    far_other, grads = lax.optimization_barrier((far_other, grads))
    far_beside = [send(far_other[at : at + PIECE], across) for at in range(0, RB, PIECE)]
    loss, *outs = finish_pairs(NEAR, scalars, far_other, emb, grads, loss, images, texts)
    grads, loss = add_pairs(FAR, scalars, far_beside, emb, grads, loss)
    grads, loss = add_pairs(FAR, scalars, [near_head_other], emb, grads, loss)
    row_loss, image_grad, text_grad = finish_pairs(
        FAR, scalars, near_tail_other, emb, grads, loss, images, texts, outs
    )
    return (row_loss, image_grad, text_grad)


def solution(mesh):
    placed = (P("blk", None), P("blk", None), P(), P())
    return jax.shard_map(
        per_device,
        mesh=mesh,
        in_specs=placed,
        out_specs=(P("blk"), P("blk", None), P("blk", None)),
        check_vma=False,
    )
```

```python
import functools

import jax
import jax.numpy as jnp
from jax import lax
from jax.experimental import pallas as pl
from jax.experimental.pallas import tpu as pltpu
from jax.sharding import PartitionSpec as P

STEPS = 3
EPS = 1e-12
RB = 768
D = 1152
TILE = 256
LANES = 128
PARTS = RB // TILE
VMEM_LIMIT = 16 * 1024 * 1024
CUT = 400
PIECE = 256
NEAR, FAR = 0, 1

ROWS_BY_COLS = (((1,), (1,)), ((), ()))
TRANSPOSED = (((0,), (0,)), ((), ()))

SCALARS = pl.BlockSpec(memory_space=pltpu.SMEM)
RESIDENT = pl.BlockSpec(memory_space=pltpu.VMEM)
ANYWHERE = pl.BlockSpec(memory_space=pl.ANY)
NO_COST = pl.CostEstimate(flops=1, bytes_accessed=1, transcendentals=0)


def kept(array):
    return pltpu.with_memory_space_constraint(array, pltpu.VMEM)


def in_hbm(array):
    return pltpu.with_memory_space_constraint(array, pltpu.HBM)


def tile(part):
    return slice(part * TILE, (part + 1) * TILE)


def normalize(raw):
    widened = raw.astype(jnp.float32)
    inverse = lax.rsqrt(jnp.sum(widened * widened, axis=1, keepdims=True) + EPS)
    return (widened * inverse, inverse)


def matmul(a, b, dims=(((1,), (0,)), ((), ()))):
    return lax.dot_general(a, b, dims, preferred_element_type=jnp.float32)


def scale_row(log_scale, width):
    return jnp.exp(jnp.full((1, width), log_scale[0], jnp.float32))


def lane_sums(values):
    total = values[:, :LANES]
    for start in range(LANES, values.shape[1], LANES):
        total = total + values[:, start : start + LANES]
    return total


def softplus_and_slope(signed):
    raised = jnp.exp(signed)
    slope = raised / ((1.0 + raised) * RB)
    return jnp.log1p(raised), slope


def copy_if(condition, source, target, sem):
    @pl.when(condition)
    def _():
        pltpu.make_async_copy(source, target, sem).start()


def pick_kernel(odd, images, texts, far, sem):
    copy_if(odd[0] == 1, texts, far, sem)
    copy_if(odd[0] == 0, images, far, sem)
    pltpu.make_async_copy(images, far, sem).wait()


def pick(odd, images, texts):
    return pl.pallas_call(
        pick_kernel,
        in_specs=[SCALARS, ANYWHERE, ANYWHERE],
        out_specs=RESIDENT,
        out_shape=pltpu.VMEM((RB, D), jnp.bfloat16),
        scratch_shapes=[pltpu.SemaphoreType.DMA],
        cost_estimate=NO_COST,
        name="pick",
    )(odd, in_hbm(images), in_hbm(texts))


def embed(raw):
    return normalize(raw)[0].astype(jnp.bfloat16)


def prepare_kernel(odd, images, texts, far, emb, near_head, near_tail, sems):
    head, tail = pl.ds(0, CUT), pl.ds(CUT, RB - CUT)
    copy_if(odd[0] == 1, images.at[head], near_head, sems.at[0])
    copy_if(odd[0] == 0, texts.at[head], near_head, sems.at[0])
    copy_if(odd[0] == 1, images.at[tail], near_tail, sems.at[1])
    copy_if(odd[0] == 0, texts.at[tail], near_tail, sems.at[1])
    for part in range(PARTS):
        emb[FAR, tile(part)] = embed(far[tile(part)])
    pltpu.make_async_copy(images.at[head], near_head, sems.at[0]).wait()
    pltpu.make_async_copy(images.at[tail], near_tail, sems.at[1]).wait()
    emb[NEAR, :CUT] = embed(near_head[...])
    emb[NEAR, CUT:] = embed(near_tail[...])


def prepare(odd, images, texts, far):
    return pl.pallas_call(
        prepare_kernel,
        in_specs=[SCALARS, ANYWHERE, ANYWHERE, RESIDENT],
        out_specs=[RESIDENT] * 3,
        out_shape=[
            pltpu.VMEM((2, RB, D), jnp.bfloat16),
            pltpu.VMEM((CUT, D), jnp.bfloat16),
            pltpu.VMEM((RB - CUT, D), jnp.bfloat16),
        ],
        scratch_shapes=[pltpu.SemaphoreType.DMA((2,))],
        compiler_params=pltpu.CompilerParams(vmem_limit_bytes=VMEM_LIMIT),
        cost_estimate=NO_COST,
        name="prepare",
    )(odd, in_hbm(images), in_hbm(texts), kept(far))


def own_kernel(odd, log_scale, logit_bias, emb, grads, loss, slopes):
    scale_tile, scale_wide = scale_row(log_scale, TILE), scale_row(log_scale, D)
    row_ids = lax.broadcasted_iota(jnp.int32, (TILE, TILE), 0)
    col_ids = lax.broadcasted_iota(jnp.int32, (TILE, TILE), 1)
    images, texts = 1 - odd[0], odd[0]
    for row in range(PARTS):
        losses = jnp.zeros((TILE, LANES), jnp.float32)
        for col in range(PARTS):
            logits = (
                scale_tile * matmul(emb[images, tile(row)], emb[texts, tile(col)], ROWS_BY_COLS)
                + logit_bias[0]
            )
            if row == col:
                same = row_ids == col_ids
                terms, slope = softplus_and_slope(jnp.where(same, -logits, logits))
                slope = jnp.where(same, -slope, slope)
            else:
                terms, slope = softplus_and_slope(logits)
            losses = losses + lane_sums(terms)
            slopes[tile(row), tile(col)] = slope.astype(jnp.bfloat16)
        loss[tile(row)] = losses
        grads[images, tile(row)] = scale_wide * matmul(slopes[tile(row)], emb[texts])
    for col in range(PARTS):
        grads[texts, tile(col)] = scale_wide * matmul(
            slopes[:, tile(col)], emb[images], TRANSPOSED
        )


def own_pairs(odd, log_scale, logit_bias, emb):
    return pl.pallas_call(
        own_kernel,
        in_specs=[SCALARS] * 3 + [RESIDENT],
        out_specs=[RESIDENT] * 2,
        out_shape=[
            pltpu.VMEM((2, RB, D), jnp.float32),
            pltpu.VMEM((RB, LANES), jnp.float32),
        ],
        scratch_shapes=[pltpu.VMEM((RB, RB), jnp.bfloat16)],
        compiler_params=pltpu.CompilerParams(vmem_limit_bytes=VMEM_LIMIT),
        cost_estimate=NO_COST,
        name="own_pairs",
    )(odd, log_scale, logit_bias, kept(emb))


def padded(count):
    return -(-count // LANES) * LANES


def embed_all(others, other_emb):
    start = 0
    for other in others:
        count = other.shape[0]
        for at in range(0, count, LANES):
            step = min(LANES, count - at)
            other_emb[start : start + step] = embed(other[at : at + step])
            start += step
    if start < other_emb.shape[0]:
        other_emb[start:] = jnp.zeros((other_emb.shape[0] - start, D), jnp.bfloat16)
    return start


def score(side, has_loss, log_scale, logit_bias, emb, loss_in, loss, other_emb, slopes, valid):
    count = other_emb.shape[0]
    step = RB if count >= RB else TILE
    for row in range(0, RB, step):
        rows = slice(row, row + step)
        losses = jnp.zeros((step, LANES), jnp.float32)
        for start in range(0, count, TILE):
            cols = slice(start, min(start + TILE, count))
            width = cols.stop - start
            logits = (
                scale_row(log_scale, width)
                * matmul(emb[side, rows], other_emb[cols], ROWS_BY_COLS)
                + logit_bias[0]
            )
            terms, slope = softplus_and_slope(logits)
            if cols.stop > valid:
                ids = lax.broadcasted_iota(jnp.int32, (step, width), 1)
                terms = jnp.where(ids < valid - start, terms, 0.0)
            losses = losses + lane_sums(terms)
            slopes[rows, cols] = slope.astype(jnp.bfloat16)
        loss[rows] = loss_in[rows] + jnp.where(has_loss, losses, 0.0)


def add_kernel(*refs, side, pieces, fetch):
    odd, log_scale, logit_bias, *others = refs[: 3 + pieces]
    emb, grads_in, loss_in, *refs = refs[3 + pieces :]
    has_loss = odd[0] == (1 if side == NEAR else 0)
    if fetch:
        images, texts, grads, loss, raw, other_emb, slopes, raw_sem = refs
        copy_if(has_loss, images, raw, raw_sem)
        copy_if(jnp.logical_not(has_loss), texts, raw, raw_sem)
    else:
        grads, loss, other_emb, slopes = refs
    valid = embed_all(others, other_emb)
    score(side, has_loss, log_scale, logit_bias, emb, loss_in, loss, other_emb, slopes, valid)
    scale_wide = scale_row(log_scale, D)
    step = RB if other_emb.shape[0] >= RB else TILE
    for row in range(0, RB, step):
        rows = slice(row, row + step)
        grads[side, rows] = grads_in[side, rows] + scale_wide * matmul(
            slopes[rows], other_emb[...]
        )
    if fetch:
        pltpu.make_async_copy(images, raw, raw_sem).wait()


def finish_kernel(*refs, side):
    odd, log_scale, logit_bias, other, emb, grads, loss_in, raw = refs[:8]
    if side == FAR:
        refs = refs[2:]
    loss, image_grad, text_grad, *scratch = refs[8:]
    other_emb, slopes, finished, out_sems = scratch[:4]
    of_images = odd[0] == (1 if side == NEAR else 0)
    valid = embed_all([other], other_emb)
    sums = loss if side == NEAR else scratch[4]
    score(side, of_images, log_scale, logit_bias, emb, loss_in, sums, other_emb, slopes, valid)
    scale_wide = scale_row(log_scale, D)

    def accumulate(rows):
        finished[rows] = grads[side, rows] + scale_wide * matmul(slopes[rows], other_emb[...])

    def finish(here):
        total = finished[here]
        unit, inverse = normalize(raw[here])
        finished[here] = (total - unit * jnp.sum(unit * total, axis=1, keepdims=True)) * inverse

    if side == NEAR:
        accumulate(slice(0, RB))
    for row in range(PARTS):
        here = tile(row)
        if side == FAR:
            accumulate(here)
        finish(here)
        copy_if(of_images, finished.at[here], image_grad.at[here], out_sems.at[row])
        copy_if(
            jnp.logical_not(of_images), finished.at[here], text_grad.at[here], out_sems.at[row]
        )
    if side == FAR:
        for row in range(PARTS):
            loss[tile(row)] = jnp.sum(sums[tile(row)].T, axis=0) * (1.0 / (STEPS * RB))
    for row in range(PARTS):
        here = tile(row)
        pltpu.make_async_copy(finished.at[here], image_grad.at[here], out_sems.at[row]).wait()


def score_scratch(count):
    return [
        pltpu.VMEM((padded(count), D), jnp.bfloat16),
        pltpu.VMEM((RB, padded(count)), jnp.bfloat16),
    ]


def add_pairs(side, scalars, others, emb, grads, loss, fetch=()):
    count = sum(other.shape[0] for other in others)
    at = 4 + len(others)
    raw = pltpu.VMEM((RB, D), jnp.bfloat16)
    return pl.pallas_call(
        functools.partial(add_kernel, side=side, pieces=len(others), fetch=bool(fetch)),
        in_specs=[SCALARS] * 3 + [RESIDENT] * (3 + len(others)) + [ANYWHERE] * len(fetch),
        out_specs=[RESIDENT] * (3 if fetch else 2),
        out_shape=[
            pltpu.VMEM(grads.shape, jnp.float32),
            pltpu.VMEM(loss.shape, jnp.float32),
        ]
        + ([raw] if fetch else []),
        scratch_shapes=score_scratch(count) + ([pltpu.SemaphoreType.DMA] if fetch else []),
        input_output_aliases={at: 0, at + 1: 1},
        compiler_params=pltpu.CompilerParams(vmem_limit_bytes=VMEM_LIMIT),
        cost_estimate=NO_COST,
        name="add_pairs",
    )(
        *scalars,
        *map(kept, others),
        kept(emb),
        kept(grads),
        kept(loss),
        *map(in_hbm, fetch),
    )


def finish_pairs(side, scalars, other, emb, grads, loss, raw, outs=()):
    count = other.shape[0]
    last = side == FAR
    return pl.pallas_call(
        functools.partial(finish_kernel, side=side),
        in_specs=[SCALARS] * 3 + [RESIDENT] * 5 + [ANYWHERE] * len(outs),
        out_specs=[RESIDENT, ANYWHERE, ANYWHERE],
        out_shape=[
            jax.ShapeDtypeStruct((RB,), jnp.float32)
            if last
            else pltpu.VMEM(loss.shape, jnp.float32),
            jax.ShapeDtypeStruct((RB, D), jnp.float32),
            jax.ShapeDtypeStruct((RB, D), jnp.float32),
        ],
        scratch_shapes=score_scratch(count)
        + [
            pltpu.VMEM((RB, D), jnp.float32),
            pltpu.SemaphoreType.DMA((PARTS,)),
        ]
        + ([pltpu.VMEM(loss.shape, jnp.float32)] if last else []),
        input_output_aliases={8: 1, 9: 2} if last else {6: 0},
        compiler_params=pltpu.CompilerParams(vmem_limit_bytes=VMEM_LIMIT),
        cost_estimate=NO_COST,
        name="finish_pairs",
    )(
        *scalars,
        kept(other),
        kept(emb),
        kept(grads),
        kept(loss),
        kept(raw),
        *outs,
    )


def per_device(images, texts, log_scale, logit_bias):
    count = lax.axis_size("blk")
    odd = (lax.axis_index("blk") % 2).astype(jnp.int32)[None]
    scalars = (odd, log_scale, logit_bias)

    first = [(i, (i + 2) % count if i % 2 else (i - 2) % count) for i in range(count)]
    second = [(i, (i + 1) % count if i % 2 else (i - 1) % count) for i in range(count)]
    across = [(i, i ^ 1) for i in range(count)]

    def send(block, pairs):
        return lax.ppermute(block, "blk", pairs)

    far = pick(odd, images, texts)
    far_other = send(far, first)
    emb, near_head, near_tail = prepare(odd, images, texts, far)
    beside_head = send(near_head, across)
    beside_tail = send(near_tail, across)
    beside_head, beside_tail, emb = lax.optimization_barrier((beside_head, beside_tail, emb))
    near_head_other = send(beside_head, second)
    grads, loss = own_pairs(*scalars, emb)
    beside_tail, grads = lax.optimization_barrier((beside_tail, grads))
    near_tail_other = send(beside_tail, second)
    grads, loss, raw = add_pairs(
        NEAR, scalars, [beside_head, beside_tail], emb, grads, loss, (images, texts)
    )
    far_other, grads = lax.optimization_barrier((far_other, grads))
    far_beside = [send(far_other[at : at + PIECE], across) for at in range(0, RB, PIECE)]
    loss, *outs = finish_pairs(NEAR, scalars, far_other, emb, grads, loss, raw)
    grads, loss, raw = add_pairs(
        FAR, scalars, [*far_beside, near_head_other], emb, grads, loss, (images, texts)
    )
    row_loss, image_grad, text_grad = finish_pairs(
        FAR, scalars, near_tail_other, emb, grads, loss, raw, outs
    )
    return (row_loss, image_grad, text_grad)


def solution(mesh):
    placed = (P("blk", None), P("blk", None), P(), P())
    return jax.shard_map(
        per_device,
        mesh=mesh,
        in_specs=placed,
        out_specs=(P("blk"), P("blk", None), P("blk", None)),
        check_vma=False,
    )
```

```python
import functools

import jax
import jax.numpy as jnp
from jax import lax
from jax.experimental import pallas as pl
from jax.experimental.pallas import tpu as pltpu
from jax.sharding import PartitionSpec as P

STEPS = 3
EPS = 1e-12
RB = 768
D = 1152
TILE = 256
LANES = 128
PARTS = RB // TILE
VMEM_LIMIT = 16 * 1024 * 1024
CUT = 400
PIECE = 256
NEAR, FAR = 0, 1

ROWS_BY_COLS = (((1,), (1,)), ((), ()))
TRANSPOSED = (((0,), (0,)), ((), ()))

SCALARS = pl.BlockSpec(memory_space=pltpu.SMEM)
RESIDENT = pl.BlockSpec(memory_space=pltpu.VMEM)
ANYWHERE = pl.BlockSpec(memory_space=pl.ANY)
NO_COST = pl.CostEstimate(flops=1, bytes_accessed=1, transcendentals=0)


def kept(array):
    return pltpu.with_memory_space_constraint(array, pltpu.VMEM)


def in_hbm(array):
    return pltpu.with_memory_space_constraint(array, pltpu.HBM)


def tile(part):
    return slice(part * TILE, (part + 1) * TILE)


def normalize(raw):
    widened = raw.astype(jnp.float32)
    inverse = lax.rsqrt(jnp.sum(widened * widened, axis=1, keepdims=True) + EPS)
    return (widened * inverse, inverse)


def matmul(a, b, dims=(((1,), (0,)), ((), ()))):
    return lax.dot_general(a, b, dims, preferred_element_type=jnp.float32)


def scale_row(log_scale, width):
    return jnp.exp(jnp.full((1, width), log_scale[0], jnp.float32))


def lane_sums(values):
    total = values[:, :LANES]
    for start in range(LANES, values.shape[1], LANES):
        total = total + values[:, start : start + LANES]
    return total


def softplus_and_slope(signed):
    raised = jnp.exp(signed)
    slope = raised / ((1.0 + raised) * RB)
    return jnp.log1p(raised), slope


def copy_if(condition, source, target, sem):
    @pl.when(condition)
    def _():
        pltpu.make_async_copy(source, target, sem).start()


def pick_kernel(odd, images, texts, far, sem):
    copy_if(odd[0] == 1, texts, far, sem)
    copy_if(odd[0] == 0, images, far, sem)
    pltpu.make_async_copy(images, far, sem).wait()


def pick(odd, images, texts):
    return pl.pallas_call(
        pick_kernel,
        in_specs=[SCALARS, ANYWHERE, ANYWHERE],
        out_specs=RESIDENT,
        out_shape=pltpu.VMEM((RB, D), jnp.bfloat16),
        scratch_shapes=[pltpu.SemaphoreType.DMA],
        cost_estimate=NO_COST,
        name="pick",
    )(odd, in_hbm(images), in_hbm(texts))


def embed(raw):
    return normalize(raw)[0].astype(jnp.bfloat16)


def prepare_kernel(odd, images, texts, far, emb, near_head, near_tail, sems):
    head, tail = pl.ds(0, CUT), pl.ds(CUT, RB - CUT)
    copy_if(odd[0] == 1, images.at[head], near_head, sems.at[0])
    copy_if(odd[0] == 0, texts.at[head], near_head, sems.at[0])
    copy_if(odd[0] == 1, images.at[tail], near_tail, sems.at[1])
    copy_if(odd[0] == 0, texts.at[tail], near_tail, sems.at[1])
    for part in range(PARTS):
        emb[FAR, tile(part)] = embed(far[tile(part)])
    pltpu.make_async_copy(images.at[head], near_head, sems.at[0]).wait()
    pltpu.make_async_copy(images.at[tail], near_tail, sems.at[1]).wait()
    emb[NEAR, :CUT] = embed(near_head[...])
    emb[NEAR, CUT:] = embed(near_tail[...])


def prepare(odd, images, texts, far):
    return pl.pallas_call(
        prepare_kernel,
        in_specs=[SCALARS, ANYWHERE, ANYWHERE, RESIDENT],
        out_specs=[RESIDENT] * 3,
        out_shape=[
            pltpu.VMEM((2, RB, D), jnp.bfloat16),
            pltpu.VMEM((CUT, D), jnp.bfloat16),
            pltpu.VMEM((RB - CUT, D), jnp.bfloat16),
        ],
        scratch_shapes=[pltpu.SemaphoreType.DMA((2,))],
        compiler_params=pltpu.CompilerParams(vmem_limit_bytes=VMEM_LIMIT),
        cost_estimate=NO_COST,
        name="prepare",
    )(odd, in_hbm(images), in_hbm(texts), kept(far))


def own_kernel(odd, log_scale, logit_bias, emb, grads, loss, slopes):
    scale_tile, scale_wide = scale_row(log_scale, TILE), scale_row(log_scale, D)
    row_ids = lax.broadcasted_iota(jnp.int32, (TILE, TILE), 0)
    col_ids = lax.broadcasted_iota(jnp.int32, (TILE, TILE), 1)
    images, texts = 1 - odd[0], odd[0]
    for row in range(PARTS):
        losses = jnp.zeros((TILE, LANES), jnp.float32)
        for col in range(PARTS):
            logits = (
                scale_tile * matmul(emb[images, tile(row)], emb[texts, tile(col)], ROWS_BY_COLS)
                + logit_bias[0]
            )
            if row == col:
                same = row_ids == col_ids
                terms, slope = softplus_and_slope(jnp.where(same, -logits, logits))
                slope = jnp.where(same, -slope, slope)
            else:
                terms, slope = softplus_and_slope(logits)
            losses = losses + lane_sums(terms)
            slopes[tile(row), tile(col)] = slope.astype(jnp.bfloat16)
        loss[tile(row)] = losses
        grads[images, tile(row)] = scale_wide * matmul(slopes[tile(row)], emb[texts])
    for col in range(PARTS):
        grads[texts, tile(col)] = scale_wide * matmul(
            slopes[:, tile(col)], emb[images], TRANSPOSED
        )


def own_pairs(odd, log_scale, logit_bias, emb):
    return pl.pallas_call(
        own_kernel,
        in_specs=[SCALARS] * 3 + [RESIDENT],
        out_specs=[RESIDENT] * 2,
        out_shape=[
            pltpu.VMEM((2, RB, D), jnp.float32),
            pltpu.VMEM((RB, LANES), jnp.float32),
        ],
        scratch_shapes=[pltpu.VMEM((RB, RB), jnp.bfloat16)],
        compiler_params=pltpu.CompilerParams(vmem_limit_bytes=VMEM_LIMIT),
        cost_estimate=NO_COST,
        name="own_pairs",
    )(odd, log_scale, logit_bias, kept(emb))


def padded(count):
    return -(-count // LANES) * LANES


def embed_all(others, other_emb):
    start = 0
    for other in others:
        count = other.shape[0]
        for at in range(0, count, LANES):
            step = min(LANES, count - at)
            other_emb[start : start + step] = embed(other[at : at + step])
            start += step
    if start < other_emb.shape[0]:
        other_emb[start:] = jnp.zeros((other_emb.shape[0] - start, D), jnp.bfloat16)
    return start


def score(side, has_loss, log_scale, logit_bias, emb, loss_in, loss, other_emb, slopes, valid):
    count = other_emb.shape[0]
    step = RB if count >= RB else TILE
    for row in range(0, RB, step):
        rows = slice(row, row + step)
        losses = jnp.zeros((step, LANES), jnp.float32)
        for start in range(0, count, TILE):
            cols = slice(start, min(start + TILE, count))
            width = cols.stop - start
            logits = (
                scale_row(log_scale, width)
                * matmul(emb[side, rows], other_emb[cols], ROWS_BY_COLS)
                + logit_bias[0]
            )
            terms, slope = softplus_and_slope(logits)
            if cols.stop > valid:
                ids = lax.broadcasted_iota(jnp.int32, (step, width), 1)
                terms = jnp.where(ids < valid - start, terms, 0.0)
            losses = losses + lane_sums(terms)
            slopes[rows, cols] = slope.astype(jnp.bfloat16)
        loss[rows] = loss_in[rows] + jnp.where(has_loss, losses, 0.0)


def row_steps(count):
    step = RB if count >= RB else TILE
    return [slice(row, row + step) for row in range(0, RB, step)]


def accumulate(side, rows, log_scale, grads, slopes, other_emb):
    return grads[side, rows] + scale_row(log_scale, D) * matmul(slopes[rows], other_emb[...])


def back_norm(total, raw):
    unit, inverse = normalize(raw)
    return (total - unit * jnp.sum(unit * total, axis=1, keepdims=True)) * inverse


def add_kernel(*refs, side, pieces, passes):
    odd, log_scale, logit_bias, *others = refs[: 3 + pieces]
    emb, grads_in, loss_in, images, texts, *refs = refs[3 + pieces :]
    has_loss = odd[0] == (1 if side == NEAR else 0)
    if passes:
        finished, grads, loss, raw, image_grad, text_grad, *refs = refs
        copy_if(jnp.logical_not(has_loss), finished, image_grad, refs[3])
        copy_if(has_loss, finished, text_grad, refs[3])
    else:
        grads, loss, raw, *refs = refs
    other_emb, slopes, raw_sem = refs[:3]
    copy_if(has_loss, images, raw, raw_sem)
    copy_if(jnp.logical_not(has_loss), texts, raw, raw_sem)
    valid = embed_all(others, other_emb)
    score(side, has_loss, log_scale, logit_bias, emb, loss_in, loss, other_emb, slopes, valid)
    for rows in row_steps(other_emb.shape[0]):
        grads[side, rows] = accumulate(side, rows, log_scale, grads_in, slopes, other_emb)
    pltpu.make_async_copy(images, raw, raw_sem).wait()
    if passes:
        pltpu.make_async_copy(finished, image_grad, refs[3]).wait()


def near_kernel(*refs):
    odd, log_scale, logit_bias, other, emb, grads, loss_in, raw, *refs = refs
    loss, finished, other_emb, slopes = refs
    valid = embed_all([other], other_emb)
    score(NEAR, odd[0] == 1, log_scale, logit_bias, emb, loss_in, loss, other_emb, slopes, valid)
    finished[...] = accumulate(NEAR, slice(0, RB), log_scale, grads, slopes, other_emb)
    for row in range(PARTS):
        finished[tile(row)] = back_norm(finished[tile(row)], raw[tile(row)])


def far_kernel(*refs):
    odd, log_scale, logit_bias, other, emb, grads, loss_in, raw, _, _, *refs = refs
    row_loss, image_grad, text_grad, other_emb, slopes, finished, sums, sems = refs
    far_images = odd[0] == 0
    valid = embed_all([other], other_emb)
    score(FAR, far_images, log_scale, logit_bias, emb, loss_in, sums, other_emb, slopes, valid)
    for row in range(PARTS):
        here = tile(row)
        total = accumulate(FAR, here, log_scale, grads, slopes, other_emb)
        finished[here] = back_norm(total, raw[here])
        copy_if(far_images, finished.at[here], image_grad.at[here], sems.at[row])
        copy_if(jnp.logical_not(far_images), finished.at[here], text_grad.at[here], sems.at[row])
    for row in range(PARTS):
        row_loss[tile(row)] = jnp.sum(sums[tile(row)].T, axis=0) * (1.0 / (STEPS * RB))
    for row in range(PARTS):
        here = tile(row)
        pltpu.make_async_copy(finished.at[here], image_grad.at[here], sems.at[row]).wait()


def score_scratch(count):
    return [
        pltpu.VMEM((padded(count), D), jnp.bfloat16),
        pltpu.VMEM((RB, padded(count)), jnp.bfloat16),
    ]


def block_grad():
    return jax.ShapeDtypeStruct((RB, D), jnp.float32)


def add_pairs(side, scalars, others, emb, grads, loss, images, texts, finished=None):
    count = sum(other.shape[0] for other in others)
    passes = finished is not None
    at = 4 + len(others)
    return pl.pallas_call(
        functools.partial(add_kernel, side=side, pieces=len(others), passes=passes),
        in_specs=[SCALARS] * 3
        + [RESIDENT] * (3 + len(others))
        + [ANYWHERE] * 2
        + [RESIDENT] * passes,
        out_specs=[RESIDENT] * 3 + [ANYWHERE] * (2 * passes),
        out_shape=[
            pltpu.VMEM(grads.shape, jnp.float32),
            pltpu.VMEM(loss.shape, jnp.float32),
            pltpu.VMEM((RB, D), jnp.bfloat16),
        ]
        + [block_grad()] * (2 * passes),
        scratch_shapes=score_scratch(count) + [pltpu.SemaphoreType.DMA] * (1 + passes),
        input_output_aliases={at: 0, at + 1: 1},
        compiler_params=pltpu.CompilerParams(vmem_limit_bytes=VMEM_LIMIT),
        cost_estimate=NO_COST,
        name="add_pairs",
    )(
        *scalars,
        *map(kept, others),
        kept(emb),
        kept(grads),
        kept(loss),
        in_hbm(images),
        in_hbm(texts),
        *([kept(finished)] if passes else []),
    )


def near_pairs(scalars, other, emb, grads, loss, raw):
    return pl.pallas_call(
        near_kernel,
        in_specs=[SCALARS] * 3 + [RESIDENT] * 5,
        out_specs=[RESIDENT] * 2,
        out_shape=[
            pltpu.VMEM(loss.shape, jnp.float32),
            pltpu.VMEM((RB, D), jnp.float32),
        ],
        scratch_shapes=score_scratch(other.shape[0]),
        input_output_aliases={6: 0},
        compiler_params=pltpu.CompilerParams(vmem_limit_bytes=VMEM_LIMIT),
        cost_estimate=NO_COST,
        name="near_pairs",
    )(*scalars, kept(other), kept(emb), kept(grads), kept(loss), kept(raw))


def far_pairs(scalars, other, emb, grads, loss, raw, outs):
    return pl.pallas_call(
        far_kernel,
        in_specs=[SCALARS] * 3 + [RESIDENT] * 5 + [ANYWHERE] * 2,
        out_specs=[RESIDENT, ANYWHERE, ANYWHERE],
        out_shape=[jax.ShapeDtypeStruct((RB,), jnp.float32), block_grad(), block_grad()],
        scratch_shapes=score_scratch(other.shape[0])
        + [
            pltpu.VMEM((RB, D), jnp.float32),
            pltpu.VMEM(loss.shape, jnp.float32),
            pltpu.SemaphoreType.DMA((PARTS,)),
        ],
        input_output_aliases={8: 1, 9: 2},
        compiler_params=pltpu.CompilerParams(vmem_limit_bytes=VMEM_LIMIT),
        cost_estimate=NO_COST,
        name="far_pairs",
    )(*scalars, kept(other), kept(emb), kept(grads), kept(loss), kept(raw), *outs)


def per_device(images, texts, log_scale, logit_bias):
    count = lax.axis_size("blk")
    odd = (lax.axis_index("blk") % 2).astype(jnp.int32)[None]
    scalars = (odd, log_scale, logit_bias)

    first = [(i, (i + 2) % count if i % 2 else (i - 2) % count) for i in range(count)]
    second = [(i, (i + 1) % count if i % 2 else (i - 1) % count) for i in range(count)]
    across = [(i, i ^ 1) for i in range(count)]

    def send(block, pairs):
        return lax.ppermute(block, "blk", pairs)

    far = pick(odd, images, texts)
    far_other = send(far, first)
    emb, near_head, near_tail = prepare(odd, images, texts, far)
    beside_head = send(near_head, across)
    beside_tail = send(near_tail, across)
    beside_head, beside_tail, emb = lax.optimization_barrier((beside_head, beside_tail, emb))
    near_head_other = send(beside_head, second)
    grads, loss = own_pairs(*scalars, emb)
    beside_tail, grads = lax.optimization_barrier((beside_tail, grads))
    near_tail_other = send(beside_tail, second)
    grads, loss, raw = add_pairs(
        NEAR, scalars, [beside_head, beside_tail], emb, grads, loss, images, texts
    )
    far_other, grads = lax.optimization_barrier((far_other, grads))
    far_beside = [send(far_other[at : at + PIECE], across) for at in range(0, RB, PIECE)]
    loss, finished = near_pairs(scalars, far_other, emb, grads, loss, raw)
    grads, loss, raw, *outs = add_pairs(
        FAR, scalars, [*far_beside, near_head_other], emb, grads, loss, images, texts, finished
    )
    row_loss, image_grad, text_grad = far_pairs(
        scalars, near_tail_other, emb, grads, loss, raw, outs
    )
    return (row_loss, image_grad, text_grad)


def solution(mesh):
    placed = (P("blk", None), P("blk", None), P(), P())
    return jax.shard_map(
        per_device,
        mesh=mesh,
        in_specs=placed,
        out_specs=(P("blk"), P("blk", None), P("blk", None)),
        check_vma=False,
    )
```

```python
import functools

import jax
import jax.numpy as jnp
from jax import lax
from jax.experimental import pallas as pl
from jax.experimental.pallas import tpu as pltpu
from jax.sharding import PartitionSpec as P

STEPS = 3
EPS = 1e-12
RB = 768
D = 1152
TILE = 256
LANES = 128
PARTS = RB // TILE
VMEM_LIMIT = 16 * 1024 * 1024
CUT = 400
PIECE = 256
NEAR, FAR = 0, 1

ROWS_BY_COLS = (((1,), (1,)), ((), ()))
TRANSPOSED = (((0,), (0,)), ((), ()))

SCALARS = pl.BlockSpec(memory_space=pltpu.SMEM)
RESIDENT = pl.BlockSpec(memory_space=pltpu.VMEM)
ANYWHERE = pl.BlockSpec(memory_space=pl.ANY)
NO_COST = pl.CostEstimate(flops=1, bytes_accessed=1, transcendentals=0)


def kept(array):
    return pltpu.with_memory_space_constraint(array, pltpu.VMEM)


def in_hbm(array):
    return pltpu.with_memory_space_constraint(array, pltpu.HBM)


def tile(part):
    return slice(part * TILE, (part + 1) * TILE)


def normalize(raw):
    widened = raw.astype(jnp.float32)
    inverse = lax.rsqrt(jnp.sum(widened * widened, axis=1, keepdims=True) + EPS)
    return (widened * inverse, inverse)


def matmul(a, b, dims=(((1,), (0,)), ((), ()))):
    return lax.dot_general(a, b, dims, preferred_element_type=jnp.float32)


def scale_row(log_scale, width):
    return jnp.exp(jnp.full((1, width), log_scale[0], jnp.float32))


def lane_sums(values):
    total = values[:, :LANES]
    for start in range(LANES, values.shape[1], LANES):
        total = total + values[:, start : start + LANES]
    return total


def softplus_and_slope(signed):
    raised = jnp.exp(signed)
    slope = raised / ((1.0 + raised) * RB)
    return jnp.log1p(raised), slope


def copy_if(condition, source, target, sem):
    @pl.when(condition)
    def _():
        pltpu.make_async_copy(source, target, sem).start()


def pick_kernel(odd, images, texts, far, sem):
    copy_if(odd[0] == 1, texts, far, sem)
    copy_if(odd[0] == 0, images, far, sem)
    pltpu.make_async_copy(images, far, sem).wait()


def pick(odd, images, texts):
    return pl.pallas_call(
        pick_kernel,
        in_specs=[SCALARS, ANYWHERE, ANYWHERE],
        out_specs=RESIDENT,
        out_shape=pltpu.VMEM((RB, D), jnp.bfloat16),
        scratch_shapes=[pltpu.SemaphoreType.DMA],
        cost_estimate=NO_COST,
        name="pick",
    )(odd, in_hbm(images), in_hbm(texts))


def embed(raw):
    return normalize(raw)[0].astype(jnp.bfloat16)


def prepare_kernel(odd, images, texts, far, emb, near_head, near_tail, sems):
    head, tail = pl.ds(0, CUT), pl.ds(CUT, RB - CUT)
    copy_if(odd[0] == 1, images.at[head], near_head, sems.at[0])
    copy_if(odd[0] == 0, texts.at[head], near_head, sems.at[0])
    copy_if(odd[0] == 1, images.at[tail], near_tail, sems.at[1])
    copy_if(odd[0] == 0, texts.at[tail], near_tail, sems.at[1])
    for part in range(PARTS):
        emb[FAR, tile(part)] = embed(far[tile(part)])
    pltpu.make_async_copy(images.at[head], near_head, sems.at[0]).wait()
    pltpu.make_async_copy(images.at[tail], near_tail, sems.at[1]).wait()
    emb[NEAR, :CUT] = embed(near_head[...])
    emb[NEAR, CUT:] = embed(near_tail[...])


def prepare(odd, images, texts, far):
    return pl.pallas_call(
        prepare_kernel,
        in_specs=[SCALARS, ANYWHERE, ANYWHERE, RESIDENT],
        out_specs=[RESIDENT] * 3,
        out_shape=[
            pltpu.VMEM((2, RB, D), jnp.bfloat16),
            pltpu.VMEM((CUT, D), jnp.bfloat16),
            pltpu.VMEM((RB - CUT, D), jnp.bfloat16),
        ],
        scratch_shapes=[pltpu.SemaphoreType.DMA((2,))],
        compiler_params=pltpu.CompilerParams(vmem_limit_bytes=VMEM_LIMIT),
        cost_estimate=NO_COST,
        name="prepare",
    )(odd, in_hbm(images), in_hbm(texts), kept(far))


def own_kernel(odd, log_scale, logit_bias, emb, grads, loss, slopes):
    scale_tile, scale_wide = scale_row(log_scale, TILE), scale_row(log_scale, D)
    row_ids = lax.broadcasted_iota(jnp.int32, (TILE, TILE), 0)
    col_ids = lax.broadcasted_iota(jnp.int32, (TILE, TILE), 1)
    images, texts = 1 - odd[0], odd[0]
    for row in range(PARTS):
        losses = jnp.zeros((TILE, LANES), jnp.float32)
        for col in range(PARTS):
            logits = (
                scale_tile * matmul(emb[images, tile(row)], emb[texts, tile(col)], ROWS_BY_COLS)
                + logit_bias[0]
            )
            if row == col:
                same = row_ids == col_ids
                terms, slope = softplus_and_slope(jnp.where(same, -logits, logits))
                slope = jnp.where(same, -slope, slope)
            else:
                terms, slope = softplus_and_slope(logits)
            losses = losses + lane_sums(terms)
            slopes[tile(row), tile(col)] = slope.astype(jnp.bfloat16)
        loss[tile(row)] = losses
        grads[images, tile(row)] = scale_wide * matmul(slopes[tile(row)], emb[texts])
    for col in range(PARTS):
        grads[texts, tile(col)] = scale_wide * matmul(
            slopes[:, tile(col)], emb[images], TRANSPOSED
        )


def own_pairs(odd, log_scale, logit_bias, emb):
    return pl.pallas_call(
        own_kernel,
        in_specs=[SCALARS] * 3 + [RESIDENT],
        out_specs=[RESIDENT] * 2,
        out_shape=[
            pltpu.VMEM((2, RB, D), jnp.float32),
            pltpu.VMEM((RB, LANES), jnp.float32),
        ],
        scratch_shapes=[pltpu.VMEM((RB, RB), jnp.bfloat16)],
        compiler_params=pltpu.CompilerParams(vmem_limit_bytes=VMEM_LIMIT),
        cost_estimate=NO_COST,
        name="own_pairs",
    )(odd, log_scale, logit_bias, kept(emb))


def padded(count):
    return -(-count // LANES) * LANES


def embed_all(others, other_emb):
    start = 0
    for other in others:
        count = other.shape[0]
        for at in range(0, count, LANES):
            step = min(LANES, count - at)
            other_emb[start : start + step] = embed(other[at : at + step])
            start += step
    if start < other_emb.shape[0]:
        other_emb[start:] = jnp.zeros((other_emb.shape[0] - start, D), jnp.bfloat16)
    return start


def score(side, has_loss, log_scale, logit_bias, emb, loss_in, loss, other_emb, slopes, valid):
    count = other_emb.shape[0]
    step = RB if count >= RB else TILE
    for row in range(0, RB, step):
        rows = slice(row, row + step)
        losses = jnp.zeros((step, LANES), jnp.float32)
        for start in range(0, count, TILE):
            cols = slice(start, min(start + TILE, count))
            width = cols.stop - start
            logits = (
                scale_row(log_scale, width)
                * matmul(emb[side, rows], other_emb[cols], ROWS_BY_COLS)
                + logit_bias[0]
            )
            terms, slope = softplus_and_slope(logits)
            if cols.stop > valid:
                ids = lax.broadcasted_iota(jnp.int32, (step, width), 1)
                terms = jnp.where(ids < valid - start, terms, 0.0)
            losses = losses + lane_sums(terms)
            slopes[rows, cols] = slope.astype(jnp.bfloat16)
        loss[rows] = loss_in[rows] + jnp.where(has_loss, losses, 0.0)


def row_steps(count):
    step = RB if count >= RB else TILE
    return [slice(row, row + step) for row in range(0, RB, step)]


def accumulate(side, rows, log_scale, grads, slopes, other_emb):
    return grads[side, rows] + scale_row(log_scale, D) * matmul(slopes[rows], other_emb[...])


def back_norm(total, raw):
    widened = raw.astype(jnp.float32)
    inverse = lax.rsqrt(jnp.sum(widened * widened, axis=1, keepdims=True) + EPS)
    along = jnp.sum(widened * total, axis=1, keepdims=True)
    return total * inverse - widened * (inverse * (inverse * (inverse * along)))


def add_kernel(*refs, side, pieces, passes):
    odd, log_scale, logit_bias, *others = refs[: 3 + pieces]
    emb, grads_in, loss_in, images, texts, *refs = refs[3 + pieces :]
    has_loss = odd[0] == (1 if side == NEAR else 0)
    if passes:
        finished, grads, loss, raw, image_grad, text_grad, *refs = refs
        copy_if(jnp.logical_not(has_loss), finished, image_grad, refs[3])
        copy_if(has_loss, finished, text_grad, refs[3])
    else:
        grads, loss, raw, *refs = refs
    other_emb, slopes, raw_sem = refs[:3]
    copy_if(has_loss, images, raw, raw_sem)
    copy_if(jnp.logical_not(has_loss), texts, raw, raw_sem)
    valid = embed_all(others, other_emb)
    score(side, has_loss, log_scale, logit_bias, emb, loss_in, loss, other_emb, slopes, valid)
    for rows in row_steps(other_emb.shape[0]):
        grads[side, rows] = accumulate(side, rows, log_scale, grads_in, slopes, other_emb)
    pltpu.make_async_copy(images, raw, raw_sem).wait()
    if passes:
        pltpu.make_async_copy(finished, image_grad, refs[3]).wait()


def near_kernel(*refs):
    odd, log_scale, logit_bias, other, emb, grads, loss_in, raw, *refs = refs
    loss, finished, other_emb, slopes = refs
    valid = embed_all([other], other_emb)
    score(NEAR, odd[0] == 1, log_scale, logit_bias, emb, loss_in, loss, other_emb, slopes, valid)
    finished[...] = accumulate(NEAR, slice(0, RB), log_scale, grads, slopes, other_emb)
    for row in range(PARTS):
        finished[tile(row)] = back_norm(finished[tile(row)], raw[tile(row)])


def far_kernel(*refs):
    odd, log_scale, logit_bias, other, emb, grads, loss_in, raw, _, _, *refs = refs
    row_loss, image_grad, text_grad, other_emb, slopes, finished, sums, sems = refs
    far_images = odd[0] == 0
    valid = embed_all([other], other_emb)
    score(FAR, far_images, log_scale, logit_bias, emb, loss_in, sums, other_emb, slopes, valid)
    for row in range(PARTS):
        here = tile(row)
        total = accumulate(FAR, here, log_scale, grads, slopes, other_emb)
        finished[here] = back_norm(total, raw[here])
        copy_if(far_images, finished.at[here], image_grad.at[here], sems.at[row])
        copy_if(jnp.logical_not(far_images), finished.at[here], text_grad.at[here], sems.at[row])
    for row in range(PARTS):
        row_loss[tile(row)] = jnp.sum(sums[tile(row)].T, axis=0) * (1.0 / (STEPS * RB))
    for row in range(PARTS):
        here = tile(row)
        pltpu.make_async_copy(finished.at[here], image_grad.at[here], sems.at[row]).wait()


def score_scratch(count):
    return [
        pltpu.VMEM((padded(count), D), jnp.bfloat16),
        pltpu.VMEM((RB, padded(count)), jnp.bfloat16),
    ]


def block_grad():
    return jax.ShapeDtypeStruct((RB, D), jnp.float32)


def add_pairs(side, scalars, others, emb, grads, loss, images, texts, finished=None):
    count = sum(other.shape[0] for other in others)
    passes = finished is not None
    at = 4 + len(others)
    return pl.pallas_call(
        functools.partial(add_kernel, side=side, pieces=len(others), passes=passes),
        in_specs=[SCALARS] * 3
        + [RESIDENT] * (3 + len(others))
        + [ANYWHERE] * 2
        + [RESIDENT] * passes,
        out_specs=[RESIDENT] * 3 + [ANYWHERE] * (2 * passes),
        out_shape=[
            pltpu.VMEM(grads.shape, jnp.float32),
            pltpu.VMEM(loss.shape, jnp.float32),
            pltpu.VMEM((RB, D), jnp.bfloat16),
        ]
        + [block_grad()] * (2 * passes),
        scratch_shapes=score_scratch(count) + [pltpu.SemaphoreType.DMA] * (1 + passes),
        input_output_aliases={at: 0, at + 1: 1},
        compiler_params=pltpu.CompilerParams(vmem_limit_bytes=VMEM_LIMIT),
        cost_estimate=NO_COST,
        name="add_pairs",
    )(
        *scalars,
        *map(kept, others),
        kept(emb),
        kept(grads),
        kept(loss),
        in_hbm(images),
        in_hbm(texts),
        *([kept(finished)] if passes else []),
    )


def near_pairs(scalars, other, emb, grads, loss, raw):
    return pl.pallas_call(
        near_kernel,
        in_specs=[SCALARS] * 3 + [RESIDENT] * 5,
        out_specs=[RESIDENT] * 2,
        out_shape=[
            pltpu.VMEM(loss.shape, jnp.float32),
            pltpu.VMEM((RB, D), jnp.float32),
        ],
        scratch_shapes=score_scratch(other.shape[0]),
        input_output_aliases={6: 0},
        compiler_params=pltpu.CompilerParams(vmem_limit_bytes=VMEM_LIMIT),
        cost_estimate=NO_COST,
        name="near_pairs",
    )(*scalars, kept(other), kept(emb), kept(grads), kept(loss), kept(raw))


def far_pairs(scalars, other, emb, grads, loss, raw, outs):
    return pl.pallas_call(
        far_kernel,
        in_specs=[SCALARS] * 3 + [RESIDENT] * 5 + [ANYWHERE] * 2,
        out_specs=[RESIDENT, ANYWHERE, ANYWHERE],
        out_shape=[jax.ShapeDtypeStruct((RB,), jnp.float32), block_grad(), block_grad()],
        scratch_shapes=score_scratch(other.shape[0])
        + [
            pltpu.VMEM((RB, D), jnp.float32),
            pltpu.VMEM(loss.shape, jnp.float32),
            pltpu.SemaphoreType.DMA((PARTS,)),
        ],
        input_output_aliases={8: 1, 9: 2},
        compiler_params=pltpu.CompilerParams(vmem_limit_bytes=VMEM_LIMIT),
        cost_estimate=NO_COST,
        name="far_pairs",
    )(*scalars, kept(other), kept(emb), kept(grads), kept(loss), kept(raw), *outs)


def per_device(images, texts, log_scale, logit_bias):
    count = lax.axis_size("blk")
    odd = (lax.axis_index("blk") % 2).astype(jnp.int32)[None]
    scalars = (odd, log_scale, logit_bias)

    first = [(i, (i + 2) % count if i % 2 else (i - 2) % count) for i in range(count)]
    second = [(i, (i + 1) % count if i % 2 else (i - 1) % count) for i in range(count)]
    across = [(i, i ^ 1) for i in range(count)]

    def send(block, pairs):
        return lax.ppermute(block, "blk", pairs)

    far = pick(odd, images, texts)
    far_other = send(far, first)
    emb, near_head, near_tail = prepare(odd, images, texts, far)
    beside_head = send(near_head, across)
    beside_tail = send(near_tail, across)
    beside_head, beside_tail, emb = lax.optimization_barrier((beside_head, beside_tail, emb))
    near_head_other = send(beside_head, second)
    grads, loss = own_pairs(*scalars, emb)
    beside_tail, grads = lax.optimization_barrier((beside_tail, grads))
    near_tail_other = send(beside_tail, second)
    grads, loss, raw = add_pairs(
        NEAR, scalars, [beside_head, beside_tail], emb, grads, loss, images, texts
    )
    far_other, grads = lax.optimization_barrier((far_other, grads))
    far_beside = [send(far_other[at : at + PIECE], across) for at in range(0, RB, PIECE)]
    loss, finished = near_pairs(scalars, far_other, emb, grads, loss, raw)
    grads, loss, raw, *outs = add_pairs(
        FAR, scalars, [*far_beside, near_head_other], emb, grads, loss, images, texts, finished
    )
    row_loss, image_grad, text_grad = far_pairs(
        scalars, near_tail_other, emb, grads, loss, raw, outs
    )
    return (row_loss, image_grad, text_grad)


def solution(mesh):
    placed = (P("blk", None), P("blk", None), P(), P())
    return jax.shard_map(
        per_device,
        mesh=mesh,
        in_specs=placed,
        out_specs=(P("blk"), P("blk", None), P("blk", None)),
        check_vma=False,
    )
```

```python
import functools

import jax
import jax.numpy as jnp
from jax import lax
from jax.experimental import pallas as pl
from jax.experimental.pallas import tpu as pltpu
from jax.sharding import PartitionSpec as P

STEPS = 3
EPS = 1e-12
RB = 768
D = 1152
TILE = 256
LANES = 128
PARTS = RB // TILE
VMEM_LIMIT = 16 * 1024 * 1024
CUT = 400
PIECE = 256
NEAR, FAR = 0, 1

ROWS_BY_COLS = (((1,), (1,)), ((), ()))
TRANSPOSED = (((0,), (0,)), ((), ()))

SCALARS = pl.BlockSpec(memory_space=pltpu.SMEM)
RESIDENT = pl.BlockSpec(memory_space=pltpu.VMEM)
ANYWHERE = pl.BlockSpec(memory_space=pl.ANY)
NO_COST = pl.CostEstimate(flops=1, bytes_accessed=1, transcendentals=0)


def kept(array):
    return pltpu.with_memory_space_constraint(array, pltpu.VMEM)


def in_hbm(array):
    return pltpu.with_memory_space_constraint(array, pltpu.HBM)


def tile(part):
    return slice(part * TILE, (part + 1) * TILE)


def normalize(raw):
    widened = raw.astype(jnp.float32)
    inverse = lax.rsqrt(jnp.sum(widened * widened, axis=1, keepdims=True) + EPS)
    return (widened * inverse, inverse)


def matmul(a, b, dims=(((1,), (0,)), ((), ()))):
    return lax.dot_general(a, b, dims, preferred_element_type=jnp.float32)


def scale_row(log_scale, width):
    return jnp.exp(jnp.full((1, width), log_scale[0], jnp.float32))


def lane_sums(values):
    total = values[:, :LANES]
    for start in range(LANES, values.shape[1], LANES):
        total = total + values[:, start : start + LANES]
    return total


def softplus_and_slope(signed):
    raised = jnp.exp(signed)
    slope = raised / ((1.0 + raised) * RB)
    return jnp.log1p(raised), slope


def copy_if(condition, source, target, sem):
    @pl.when(condition)
    def _():
        pltpu.make_async_copy(source, target, sem).start()


def pick_kernel(odd, images, texts, far, sems):
    pieces = [pl.ds(start, LANES) for start in range(0, RB, LANES)]

    @pl.when(odd[0] == 1)
    def _():
        for at, here in enumerate(pieces):
            pltpu.make_async_copy(texts.at[here], far.at[here], sems.at[at]).start()

    @pl.when(odd[0] == 0)
    def _():
        for at, here in enumerate(pieces):
            pltpu.make_async_copy(images.at[here], far.at[here], sems.at[at]).start()

    for at, here in enumerate(pieces):
        pltpu.make_async_copy(images.at[here], far.at[here], sems.at[at]).wait()


def pick(odd, images, texts):
    return pl.pallas_call(
        pick_kernel,
        in_specs=[SCALARS, ANYWHERE, ANYWHERE],
        out_specs=RESIDENT,
        out_shape=pltpu.VMEM((RB, D), jnp.bfloat16),
        scratch_shapes=[pltpu.SemaphoreType.DMA((RB // LANES,))],
        cost_estimate=NO_COST,
        name="pick",
    )(odd, in_hbm(images), in_hbm(texts))


def embed(raw):
    return normalize(raw)[0].astype(jnp.bfloat16)


def prepare_kernel(odd, images, texts, far, emb, near_head, near_tail, sems):
    head, tail = pl.ds(0, CUT), pl.ds(CUT, RB - CUT)
    copy_if(odd[0] == 1, images.at[head], near_head, sems.at[0])
    copy_if(odd[0] == 0, texts.at[head], near_head, sems.at[0])
    copy_if(odd[0] == 1, images.at[tail], near_tail, sems.at[1])
    copy_if(odd[0] == 0, texts.at[tail], near_tail, sems.at[1])
    for part in range(PARTS):
        emb[FAR, tile(part)] = embed(far[tile(part)])
    pltpu.make_async_copy(images.at[head], near_head, sems.at[0]).wait()
    pltpu.make_async_copy(images.at[tail], near_tail, sems.at[1]).wait()
    emb[NEAR, :CUT] = embed(near_head[...])
    emb[NEAR, CUT:] = embed(near_tail[...])


def prepare(odd, images, texts, far):
    return pl.pallas_call(
        prepare_kernel,
        in_specs=[SCALARS, ANYWHERE, ANYWHERE, RESIDENT],
        out_specs=[RESIDENT] * 3,
        out_shape=[
            pltpu.VMEM((2, RB, D), jnp.bfloat16),
            pltpu.VMEM((CUT, D), jnp.bfloat16),
            pltpu.VMEM((RB - CUT, D), jnp.bfloat16),
        ],
        scratch_shapes=[pltpu.SemaphoreType.DMA((2,))],
        compiler_params=pltpu.CompilerParams(vmem_limit_bytes=VMEM_LIMIT),
        cost_estimate=NO_COST,
        name="prepare",
    )(odd, in_hbm(images), in_hbm(texts), kept(far))


def own_kernel(odd, log_scale, logit_bias, emb, grads, loss, slopes):
    scale_tile, scale_wide = scale_row(log_scale, TILE), scale_row(log_scale, D)
    row_ids = lax.broadcasted_iota(jnp.int32, (TILE, TILE), 0)
    col_ids = lax.broadcasted_iota(jnp.int32, (TILE, TILE), 1)
    images, texts = 1 - odd[0], odd[0]
    for row in range(PARTS):
        losses = jnp.zeros((TILE, LANES), jnp.float32)
        for col in range(PARTS):
            logits = (
                scale_tile * matmul(emb[images, tile(row)], emb[texts, tile(col)], ROWS_BY_COLS)
                + logit_bias[0]
            )
            if row == col:
                same = row_ids == col_ids
                terms, slope = softplus_and_slope(jnp.where(same, -logits, logits))
                slope = jnp.where(same, -slope, slope)
            else:
                terms, slope = softplus_and_slope(logits)
            losses = losses + lane_sums(terms)
            slopes[tile(row), tile(col)] = slope.astype(jnp.bfloat16)
        loss[tile(row)] = losses
        grads[images, tile(row)] = scale_wide * matmul(slopes[tile(row)], emb[texts])
    for col in range(PARTS):
        grads[texts, tile(col)] = scale_wide * matmul(
            slopes[:, tile(col)], emb[images], TRANSPOSED
        )


def own_pairs(odd, log_scale, logit_bias, emb):
    return pl.pallas_call(
        own_kernel,
        in_specs=[SCALARS] * 3 + [RESIDENT],
        out_specs=[RESIDENT] * 2,
        out_shape=[
            pltpu.VMEM((2, RB, D), jnp.float32),
            pltpu.VMEM((RB, LANES), jnp.float32),
        ],
        scratch_shapes=[pltpu.VMEM((RB, RB), jnp.bfloat16)],
        compiler_params=pltpu.CompilerParams(vmem_limit_bytes=VMEM_LIMIT),
        cost_estimate=NO_COST,
        name="own_pairs",
    )(odd, log_scale, logit_bias, kept(emb))


def padded(count):
    return -(-count // LANES) * LANES


def embed_all(others, other_emb):
    start = 0
    for other in others:
        count = other.shape[0]
        for at in range(0, count, LANES):
            step = min(LANES, count - at)
            other_emb[start : start + step] = embed(other[at : at + step])
            start += step
    if start < other_emb.shape[0]:
        other_emb[start:] = jnp.zeros((other_emb.shape[0] - start, D), jnp.bfloat16)
    return start


def score(side, has_loss, log_scale, logit_bias, emb, loss_in, loss, other_emb, slopes, valid):
    count = other_emb.shape[0]
    step = RB if count >= RB else TILE
    for row in range(0, RB, step):
        rows = slice(row, row + step)
        losses = jnp.zeros((step, LANES), jnp.float32)
        for start in range(0, count, TILE):
            cols = slice(start, min(start + TILE, count))
            width = cols.stop - start
            logits = (
                scale_row(log_scale, width)
                * matmul(emb[side, rows], other_emb[cols], ROWS_BY_COLS)
                + logit_bias[0]
            )
            terms, slope = softplus_and_slope(logits)
            if cols.stop > valid:
                ids = lax.broadcasted_iota(jnp.int32, (step, width), 1)
                terms = jnp.where(ids < valid - start, terms, 0.0)
            losses = losses + lane_sums(terms)
            slopes[rows, cols] = slope.astype(jnp.bfloat16)
        loss[rows] = loss_in[rows] + jnp.where(has_loss, losses, 0.0)


def row_steps(count):
    step = RB if count >= RB else TILE
    return [slice(row, row + step) for row in range(0, RB, step)]


def accumulate(side, rows, log_scale, grads, slopes, other_emb):
    return grads[side, rows] + scale_row(log_scale, D) * matmul(slopes[rows], other_emb[...])


def back_norm(total, raw):
    widened = raw.astype(jnp.float32)
    inverse = lax.rsqrt(jnp.sum(widened * widened, axis=1, keepdims=True) + EPS)
    along = jnp.sum(widened * total, axis=1, keepdims=True)
    return total * inverse - widened * (inverse * (inverse * (inverse * along)))


def add_kernel(*refs, side, pieces, passes):
    odd, log_scale, logit_bias, *others = refs[: 3 + pieces]
    emb, grads_in, loss_in, images, texts, *refs = refs[3 + pieces :]
    has_loss = odd[0] == (1 if side == NEAR else 0)
    if passes:
        finished, grads, loss, raw, image_grad, text_grad, *refs = refs
        copy_if(jnp.logical_not(has_loss), finished, image_grad, refs[3])
        copy_if(has_loss, finished, text_grad, refs[3])
    else:
        grads, loss, raw, *refs = refs
    other_emb, slopes, raw_sem = refs[:3]
    copy_if(has_loss, images, raw, raw_sem)
    copy_if(jnp.logical_not(has_loss), texts, raw, raw_sem)
    valid = embed_all(others, other_emb)
    score(side, has_loss, log_scale, logit_bias, emb, loss_in, loss, other_emb, slopes, valid)
    for rows in row_steps(other_emb.shape[0]):
        grads[side, rows] = accumulate(side, rows, log_scale, grads_in, slopes, other_emb)
    pltpu.make_async_copy(images, raw, raw_sem).wait()
    if passes:
        pltpu.make_async_copy(finished, image_grad, refs[3]).wait()


def near_kernel(*refs):
    odd, log_scale, logit_bias, other, emb, grads, loss_in, raw, *refs = refs
    loss, finished, other_emb, slopes = refs
    valid = embed_all([other], other_emb)
    score(NEAR, odd[0] == 1, log_scale, logit_bias, emb, loss_in, loss, other_emb, slopes, valid)
    finished[...] = accumulate(NEAR, slice(0, RB), log_scale, grads, slopes, other_emb)
    for row in range(PARTS):
        finished[tile(row)] = back_norm(finished[tile(row)], raw[tile(row)])


def far_kernel(*refs):
    odd, log_scale, logit_bias, other, emb, grads, loss_in, raw, _, _, *refs = refs
    row_loss, image_grad, text_grad, other_emb, slopes, finished, sums, sems = refs
    far_images = odd[0] == 0
    valid = embed_all([other], other_emb)
    score(FAR, far_images, log_scale, logit_bias, emb, loss_in, sums, other_emb, slopes, valid)
    for row in range(PARTS):
        here = tile(row)
        total = accumulate(FAR, here, log_scale, grads, slopes, other_emb)
        finished[here] = back_norm(total, raw[here])
        copy_if(far_images, finished.at[here], image_grad.at[here], sems.at[row])
        copy_if(jnp.logical_not(far_images), finished.at[here], text_grad.at[here], sems.at[row])
    for row in range(PARTS):
        row_loss[tile(row)] = jnp.sum(sums[tile(row)].T, axis=0) * (1.0 / (STEPS * RB))
    for row in range(PARTS):
        here = tile(row)
        pltpu.make_async_copy(finished.at[here], image_grad.at[here], sems.at[row]).wait()


def score_scratch(count):
    return [
        pltpu.VMEM((padded(count), D), jnp.bfloat16),
        pltpu.VMEM((RB, padded(count)), jnp.bfloat16),
    ]


def block_grad():
    return jax.ShapeDtypeStruct((RB, D), jnp.float32)


def add_pairs(side, scalars, others, emb, grads, loss, images, texts, finished=None):
    count = sum(other.shape[0] for other in others)
    passes = finished is not None
    at = 4 + len(others)
    return pl.pallas_call(
        functools.partial(add_kernel, side=side, pieces=len(others), passes=passes),
        in_specs=[SCALARS] * 3
        + [RESIDENT] * (3 + len(others))
        + [ANYWHERE] * 2
        + [RESIDENT] * passes,
        out_specs=[RESIDENT] * 3 + [ANYWHERE] * (2 * passes),
        out_shape=[
            pltpu.VMEM(grads.shape, jnp.float32),
            pltpu.VMEM(loss.shape, jnp.float32),
            pltpu.VMEM((RB, D), jnp.bfloat16),
        ]
        + [block_grad()] * (2 * passes),
        scratch_shapes=score_scratch(count) + [pltpu.SemaphoreType.DMA] * (1 + passes),
        input_output_aliases={at: 0, at + 1: 1},
        compiler_params=pltpu.CompilerParams(vmem_limit_bytes=VMEM_LIMIT),
        cost_estimate=NO_COST,
        name="add_pairs",
    )(
        *scalars,
        *map(kept, others),
        kept(emb),
        kept(grads),
        kept(loss),
        in_hbm(images),
        in_hbm(texts),
        *([kept(finished)] if passes else []),
    )


def near_pairs(scalars, other, emb, grads, loss, raw):
    return pl.pallas_call(
        near_kernel,
        in_specs=[SCALARS] * 3 + [RESIDENT] * 5,
        out_specs=[RESIDENT] * 2,
        out_shape=[
            pltpu.VMEM(loss.shape, jnp.float32),
            pltpu.VMEM((RB, D), jnp.float32),
        ],
        scratch_shapes=score_scratch(other.shape[0]),
        input_output_aliases={6: 0},
        compiler_params=pltpu.CompilerParams(vmem_limit_bytes=VMEM_LIMIT),
        cost_estimate=NO_COST,
        name="near_pairs",
    )(*scalars, kept(other), kept(emb), kept(grads), kept(loss), kept(raw))


def far_pairs(scalars, other, emb, grads, loss, raw, outs):
    return pl.pallas_call(
        far_kernel,
        in_specs=[SCALARS] * 3 + [RESIDENT] * 5 + [ANYWHERE] * 2,
        out_specs=[RESIDENT, ANYWHERE, ANYWHERE],
        out_shape=[jax.ShapeDtypeStruct((RB,), jnp.float32), block_grad(), block_grad()],
        scratch_shapes=score_scratch(other.shape[0])
        + [
            pltpu.VMEM((RB, D), jnp.float32),
            pltpu.VMEM(loss.shape, jnp.float32),
            pltpu.SemaphoreType.DMA((PARTS,)),
        ],
        input_output_aliases={8: 1, 9: 2},
        compiler_params=pltpu.CompilerParams(vmem_limit_bytes=VMEM_LIMIT),
        cost_estimate=NO_COST,
        name="far_pairs",
    )(*scalars, kept(other), kept(emb), kept(grads), kept(loss), kept(raw), *outs)


def per_device(images, texts, log_scale, logit_bias):
    count = lax.axis_size("blk")
    odd = (lax.axis_index("blk") % 2).astype(jnp.int32)[None]
    scalars = (odd, log_scale, logit_bias)

    first = [(i, (i + 2) % count if i % 2 else (i - 2) % count) for i in range(count)]
    second = [(i, (i + 1) % count if i % 2 else (i - 1) % count) for i in range(count)]
    across = [(i, i ^ 1) for i in range(count)]

    def send(block, pairs):
        return lax.ppermute(block, "blk", pairs)

    far = pick(odd, images, texts)
    far_other = send(far, first)
    emb, near_head, near_tail = prepare(odd, images, texts, far)
    beside_head = send(near_head, across)
    beside_tail = send(near_tail, across)
    beside_head, beside_tail, emb = lax.optimization_barrier((beside_head, beside_tail, emb))
    near_head_other = send(beside_head, second)
    grads, loss = own_pairs(*scalars, emb)
    beside_tail, grads = lax.optimization_barrier((beside_tail, grads))
    near_tail_other = send(beside_tail, second)
    grads, loss, raw = add_pairs(
        NEAR, scalars, [beside_head, beside_tail], emb, grads, loss, images, texts
    )
    far_other, grads = lax.optimization_barrier((far_other, grads))
    far_beside = [send(far_other[at : at + PIECE], across) for at in range(0, RB, PIECE)]
    loss, finished = near_pairs(scalars, far_other, emb, grads, loss, raw)
    grads, loss, raw, *outs = add_pairs(
        FAR, scalars, [*far_beside, near_head_other], emb, grads, loss, images, texts, finished
    )
    row_loss, image_grad, text_grad = far_pairs(
        scalars, near_tail_other, emb, grads, loss, raw, outs
    )
    return (row_loss, image_grad, text_grad)


def solution(mesh):
    placed = (P("blk", None), P("blk", None), P(), P())
    return jax.shard_map(
        per_device,
        mesh=mesh,
        in_specs=placed,
        out_specs=(P("blk"), P("blk", None), P("blk", None)),
        check_vma=False,
    )
```
